128 devices in a mesh: wide: 16 (over x_hi, y, core), narrow: 8 (over z, x_lo).
Axes of the slice: x: 4 (x_hi: 2, x_lo: 2; x = x_hi * 2 + x_lo), y: 4, z: 4, core: 2. Of those that a mesh axis runs over, the one named last changes fastest.
Arguments:
- tokens: bfloat16 [8192, 5120], P('wide', 'narrow'), may hold values from -400 to 400
- ln_gain: float32 [5120], replicated, may hold values from 0.1 to 1.9
- w_qkv: bfloat16 [5120, 10240], P('narrow', 'wide'), may hold values from -0.078125 to 0.078125
- q_gain: float32 [128], replicated, may hold values from 0.1 to 1.9
- k_gain: float32 [128], replicated, may hold values from 1 to 2
- stored_keys: bfloat16 [512, 256, 1024], P(('wide', 'narrow')), may hold values from -700 to 700
- stored_values: bfloat16 [512, 256, 1024], P(('wide', 'narrow')), may hold values from -6 to 6
- span_lengths: int32 [512], P(('wide', 'narrow')), may hold values from 1 to 16, 6144 in all
- fill_positions: int32 [512], P(('wide', 'narrow')), may hold values from 1 to 256, as said below
- w_out: bfloat16 [8192, 5120], P('wide', 'narrow'), may hold values from -0.25 to 0.25
Outputs:
- block_out: bfloat16 [8192, 5120], P('wide', 'narrow')
The draws below stay inside these ranges and needn't reach their ends.
Inputs may be any that keep to these rules, and one draw needn't show every extreme that they name: Slots 0 to span_lengths[s] - 1 of stream s are live, the rest of its 16 slots are padding. Frames 0 to fill_positions[s] - 1 of stream s hold its past.
All inputs are finite; a program needn't handle non-finite values. No bound on the sum of `span_lengths` on one device may be relied on, other than what follows from the above.
Results may differ from the reference program's by a relative error of at most 0.006.
The reference program's roundings to bfloat16 on the way count: a program that leaves them out, or rounds other values in their place, can miss the bound.
Values may be sent and summed in bfloat16 or wider, within the bound.
No kernel may reach another device: no remote copies, remote signals or barrier semaphores. Data moves between devices by JAX's collectives and lax.ppermute only.
A program may use at most 128 MiB of HBM per device.

```python
import math
import jax
import jax.numpy as jnp
import numpy as np
from jax import lax

D = 5120
QUERY_HEADS = 64
KEY_VALUE_HEADS = 8
HEAD_SIZE = 128
SPAN = 16
CACHE_FRAMES = 256
STREAM_TOTAL = 512
TOKENS = 8192
QKV = 10240
N_WIDE = 16


def draw_tokens(key, part):
    key = jax.random.fold_in(key, 5)
    key_noise, key_rows, key_columns = jax.random.split(key, 3)
    row_scale = jnp.exp(jax.random.uniform(key_rows, (TOKENS, 1), jnp.float32, 0.0, math.log(10.0)))
    column_index = jnp.arange(D, dtype=jnp.float32) / D
    column_rough = jnp.exp(jax.random.uniform(key_columns, (D,), jnp.float32, -1.15, 1.15))
    noise_base = jnp.clip(jax.random.normal(key_noise, (TOKENS, D), jnp.float32), -4.0, 4.0)
    column_scale = jnp.exp(math.log(3.0) * column_index) * column_rough
    return (0.5 * noise_base * row_scale * column_scale[None, :]).astype(jnp.bfloat16)


def draw_stored_keys(key, part):
    key = jax.random.fold_in(key, 9)
    key_noise = jax.random.fold_in(key, 0)
    tensor_shape = (STREAM_TOTAL, CACHE_FRAMES, KEY_VALUE_HEADS * HEAD_SIZE)
    noise_base = 1.4 * jnp.clip(jax.random.normal(key_noise, tensor_shape, jnp.float32), -4.0, 4.0)
    return noise_base.astype(jnp.bfloat16)


def draw_fill_positions(key, part):
    key = jax.random.fold_in(key, 13)
    key_fill, key_top = jax.random.split(key, 2)
    fill_draw = jax.random.randint(key_fill, (STREAM_TOTAL,), 1, CACHE_FRAMES + 1, dtype=jnp.int32)
    top_stream = jax.random.randint(key_top, (), 0, STREAM_TOTAL, dtype=jnp.int32)
    stream_index = jnp.arange(STREAM_TOTAL, dtype=jnp.int32)
    return jnp.where(stream_index == top_stream, CACHE_FRAMES, fill_draw).astype(jnp.int32)


def block_levels(rng, dims, shards, smallest, high):
    factor_of, own = 1.0, jax.random.fold_in(rng, 6)
    for dim, blocks in shards:
        steps = jnp.exp(jax.random.uniform(jax.random.fold_in(own, dim), (blocks,), jnp.float32, smallest / len(shards), high / len(shards)))
        factor_of = factor_of * jnp.repeat(steps, dims[dim] // blocks).reshape([-1 if axis == dim else 1 for axis in range(len(dims))])
    return factor_of


def split_up(number_of, total, reach, lean):
    loads = [(1 << 20) // math.isqrt(standing ** lean) + 1 for standing in range(2, number_of + 1)]
    surplus, counts = total - reach - (number_of - 1), [1] * (number_of - 1)
    while surplus > 0:
        free = [i for i in range(number_of - 1) if counts[i] < reach]
        pool, left = sum([loads[i] for i in free]), surplus
        for i in free:
            addition = min(reach - counts[i], max(1, left * loads[i] // pool), surplus)
            counts[i] = counts[i] + addition
            surplus = surplus - addition
    return np.array([reach] + counts)


def ragged(own_key, count, total, bound, skew):
    if count == 2:
        one = jax.random.randint(own_key, (), max(1, total - bound), min(bound, total - 1) + 1)
        return jnp.stack([one, total - one])
    sizes = jnp.asarray(split_up(count, total, bound, skew), jnp.int32)
    twos = (count - 1) // 2
    giver, sink = sizes[1:1 + 2 * twos:2], sizes[2:2 + 2 * twos:2]
    margin = jnp.minimum(giver - 1, bound - sink)
    moved = jax.random.randint(jax.random.fold_in(own_key, 1), (twos,), 0, 1 << 20) % (margin + 1)
    sizes = sizes.at[1:1 + 2 * twos:2].set(giver - moved).at[2:2 + 2 * twos:2].set(sink + moved)
    return sizes[jax.random.permutation(jax.random.fold_in(own_key, 2), count)]


def centred(stream_key, extent, scale, most, cuts=(), kind=jnp.bfloat16):
    level = block_levels(stream_key, extent, cuts, -0.22, 0.18) if cuts else 1.0
    result = jax.random.normal(stream_key, extent, jnp.float32) * scale * level
    return jnp.minimum(jnp.maximum(result, -most), most).astype(kind)


def setup_inputs(seed: int = 0) -> dict:
    splits = jax.random.split(jax.random.key(seed), 11)
    tokens = draw_tokens(jax.random.fold_in(splits[10], 71), 0)
    ln_gain = jnp.clip(1.0 + 0.18 * jax.random.normal(splits[1], (D,), jnp.float32), 0.1, 1.9)
    w_qkv = centred(splits[2], (D, QKV), D ** -0.5, 0.078125, ((0, 8), (1, 16)))
    q_gain = jnp.clip(1.0 + 0.18 * jax.random.normal(splits[3], (HEAD_SIZE,), jnp.float32), 0.1, 1.9)
    k_gain = jnp.clip(jnp.exp(jax.random.uniform(splits[4], (HEAD_SIZE,), jnp.float32, math.log(1.0), math.log(2.0))), 1.0, 2.0)
    stored_keys = draw_stored_keys(jax.random.fold_in(splits[10], 71), 0)
    stored_values = centred(splits[6], (STREAM_TOTAL, CACHE_FRAMES, KEY_VALUE_HEADS * HEAD_SIZE), 1.0, 6.0, ((0, 128),))
    span_lengths = ragged(splits[7], STREAM_TOTAL, STREAM_TOTAL * SPAN * 3 // 4, SPAN, 0).astype(jnp.int32)
    fill_positions = draw_fill_positions(jax.random.fold_in(splits[10], 71), 0)
    w_out = centred(splits[9], (QUERY_HEADS * HEAD_SIZE, D), (QUERY_HEADS * HEAD_SIZE // 16) ** -0.5, 0.25, ((0, 16), (1, 8)))
    return dict(tokens=tokens, ln_gain=ln_gain, w_qkv=w_qkv, q_gain=q_gain, k_gain=k_gain, stored_keys=stored_keys, stored_values=stored_values, span_lengths=span_lengths, fill_positions=fill_positions, w_out=w_out)


EPSILON = 1e-06
ROPE_BASE = 1000000.0

def head_norm(vectors, gains):
    mean_square = lax.optimization_barrier(jnp.mean(vectors * vectors, axis=-1, keepdims=True))
    return vectors * lax.rsqrt(mean_square + EPSILON) * gains

def rotate(vectors, position):
    half_dim = vectors.shape[-1] // 2
    frequency = jnp.exp(jnp.arange(half_dim, dtype=jnp.float32) * (-2.0 * math.log(ROPE_BASE) / vectors.shape[-1]))
    angles = position[:, None] * frequency[None, :]
    cosine = jnp.cos(angles)[:, None, :]
    sine_part = jnp.sin(angles)[:, None, :]
    first_half = vectors[..., :half_dim]
    second_half = vectors[..., half_dim:]
    return jnp.concatenate([first_half * cosine - second_half * sine_part, second_half * cosine + first_half * sine_part], axis=-1)

def attend(packed, squares, head_groups, q_gain, k_gain, stored_keys, stored_values, span_lengths, fill_positions):
    stream_list = span_lengths.shape[0]
    total_row_count = packed.shape[0]
    cache_slot_count = total_row_count // stream_list
    cache_frame_count = stored_keys.shape[1]
    query_group_size = QUERY_HEADS // KEY_VALUE_HEADS
    query_columns = QUERY_HEADS * HEAD_SIZE // head_groups
    key_columns = KEY_VALUE_HEADS * HEAD_SIZE // head_groups
    grouped_queries = packed.reshape(total_row_count, head_groups, query_columns + 2 * key_columns)
    query_raw = grouped_queries[:, :, :query_columns].reshape(total_row_count, QUERY_HEADS, HEAD_SIZE).astype(jnp.float32)
    unnormed_key = grouped_queries[:, :, query_columns:query_columns + key_columns].reshape(total_row_count, KEY_VALUE_HEADS, HEAD_SIZE).astype(jnp.float32)
    unnormed_value = grouped_queries[:, :, query_columns + key_columns:].reshape(total_row_count, KEY_VALUE_HEADS * HEAD_SIZE).astype(jnp.float32)
    inverse_root_mean = lax.rsqrt(squares / D + EPSILON)
    fresh_values = lax.optimization_barrier((unnormed_value * inverse_root_mean[:, None]).astype(jnp.bfloat16))
    fresh_values = fresh_values.reshape(stream_list, cache_slot_count, KEY_VALUE_HEADS, HEAD_SIZE).astype(jnp.float32)
    slot_index = jnp.arange(cache_slot_count, dtype=jnp.int32)
    position = (fill_positions[:, None] + slot_index[None, :]).reshape(total_row_count).astype(jnp.float32)
    query_rows = lax.optimization_barrier(rotate(head_norm(query_raw, q_gain), position).astype(jnp.bfloat16))
    query_rows = query_rows.reshape(stream_list, cache_slot_count, KEY_VALUE_HEADS, query_group_size, HEAD_SIZE).astype(jnp.float32)
    fresh_keys = lax.optimization_barrier(rotate(head_norm(unnormed_key, k_gain), position).astype(jnp.bfloat16))
    fresh_keys = fresh_keys.reshape(stream_list, cache_slot_count, KEY_VALUE_HEADS, HEAD_SIZE).astype(jnp.float32)
    earlier_keys = stored_keys.reshape(stream_list, cache_frame_count, KEY_VALUE_HEADS, HEAD_SIZE).astype(jnp.float32)
    earlier_values = stored_values.reshape(stream_list, cache_frame_count, KEY_VALUE_HEADS, HEAD_SIZE).astype(jnp.float32)
    score_scale = 1.0 / math.sqrt(HEAD_SIZE)
    old_scores = jnp.einsum('sckgd,sfkd->skgcf', query_rows, earlier_keys) * score_scale
    new_scores = jnp.einsum('sckgd,sjkd->skgcj', query_rows, fresh_keys) * score_scale
    frame_index = jnp.arange(cache_frame_count, dtype=jnp.int32)
    old_live = (frame_index[None, :] < fill_positions[:, None])[:, None, None, None, :]
    new_live = (slot_index[None, None, :] <= slot_index[None, :, None]) & (slot_index[None, None, :] < span_lengths[:, None, None])
    new_live = new_live[:, None, None, :, :]
    old_scores = jnp.where(old_live, old_scores, -1e+30)
    new_scores = jnp.where(new_live, new_scores, -1e+30)
    row_max = jnp.maximum(lax.optimization_barrier(jnp.max(old_scores, axis=-1, keepdims=True)), lax.optimization_barrier(jnp.max(new_scores, axis=-1, keepdims=True)))
    old_weights = jnp.exp(old_scores - row_max)
    new_weights = jnp.exp(new_scores - row_max)
    denominator = lax.optimization_barrier(jnp.sum(old_weights, axis=-1)) + lax.optimization_barrier(jnp.sum(new_weights, axis=-1))
    old_probs = lax.optimization_barrier(old_weights.astype(jnp.bfloat16)).astype(jnp.float32)
    new_probs = lax.optimization_barrier(new_weights.astype(jnp.bfloat16)).astype(jnp.float32)
    mixed_heads = jnp.einsum('skgcf,sfkd->sckgd', old_probs, earlier_values) + jnp.einsum('skgcj,sjkd->sckgd', new_probs, fresh_values)
    mixed_heads = mixed_heads / jnp.transpose(denominator, (0, 3, 1, 2))[..., None]
    query_live = (slot_index[None, :] < span_lengths[:, None])[:, :, None, None, None]
    mixed_heads = jnp.where(query_live, mixed_heads, 0.0)
    return mixed_heads.reshape(total_row_count, QUERY_HEADS * HEAD_SIZE).astype(jnp.bfloat16)

def reference(tokens, ln_gain, w_qkv, q_gain, k_gain, stored_keys, stored_values, span_lengths, fill_positions, w_out):
    token_values = tokens.astype(jnp.float32)
    normed = (token_values * ln_gain[None, :]).astype(jnp.bfloat16)
    squares = lax.optimization_barrier(jnp.sum(token_values * token_values, axis=1))
    packed = jnp.dot(normed, w_qkv, preferred_element_type=jnp.float32).astype(jnp.bfloat16)
    packed = lax.optimization_barrier(packed)
    attended = attend(packed, squares, N_WIDE, q_gain, k_gain, stored_keys, stored_values, span_lengths, fill_positions)
    return jnp.dot(attended, w_out, preferred_element_type=jnp.float32).astype(jnp.bfloat16)
```

```python
import math

import jax
import jax.numpy as jnp
from jax import lax
from jax.sharding import PartitionSpec as P

D = 5120
QUERY_HEADS = 64
KEY_VALUE_HEADS = 8
HEAD_SIZE = 128


EPSILON = 1e-06
ROPE_BASE = 1000000.0


def head_norm(vectors, gains):
    mean_square = jnp.mean(vectors * vectors, axis=-1, keepdims=True)
    return vectors * lax.rsqrt(mean_square + EPSILON) * gains


def rotate(vectors, position):
    half_dim = vectors.shape[-1] // 2
    frequency = jnp.exp(
        jnp.arange(half_dim, dtype=jnp.float32) * (-2.0 * math.log(ROPE_BASE) / vectors.shape[-1])
    )
    angles = position[:, None] * frequency[None, :]
    cosine = jnp.cos(angles)[:, None, :]
    sine_part = jnp.sin(angles)[:, None, :]
    first_half = vectors[..., :half_dim]
    second_half = vectors[..., half_dim:]
    return jnp.concatenate(
        [
            first_half * cosine - second_half * sine_part,
            second_half * cosine + first_half * sine_part,
        ],
        axis=-1,
    )


def attend(
    packed,
    own_squares,
    head_groups,
    q_gain,
    k_gain,
    stored_keys,
    stored_values,
    span_lengths,
    fill_positions,
):
    stream_list = span_lengths.shape[0]
    total_row_count = packed.shape[0]
    cache_slot_count = total_row_count // stream_list
    cache_frame_count = stored_keys.shape[1]
    query_group_size = QUERY_HEADS // KEY_VALUE_HEADS
    query_columns = QUERY_HEADS * HEAD_SIZE // head_groups
    key_columns = KEY_VALUE_HEADS * HEAD_SIZE // head_groups
    grouped_queries = packed.reshape(total_row_count, head_groups, query_columns + 2 * key_columns)
    query_raw = (
        grouped_queries[:, :, :query_columns]
        .reshape(total_row_count, QUERY_HEADS, HEAD_SIZE)
        .astype(jnp.float32)
    )
    unnormed_key = (
        grouped_queries[:, :, query_columns : query_columns + key_columns]
        .reshape(total_row_count, KEY_VALUE_HEADS, HEAD_SIZE)
        .astype(jnp.float32)
    )
    unnormed_value = (
        grouped_queries[:, :, query_columns + key_columns :]
        .reshape(total_row_count, KEY_VALUE_HEADS * HEAD_SIZE)
        .astype(jnp.float32)
    )
    inverse_root_mean = lax.rsqrt(own_squares / D + EPSILON)
    fresh_values = (
        (unnormed_value * inverse_root_mean[:, None])
        .astype(jnp.bfloat16)
        .reshape(stream_list, cache_slot_count, KEY_VALUE_HEADS, HEAD_SIZE)
    )
    slot_index = jnp.arange(cache_slot_count, dtype=jnp.int32)
    position = (
        (fill_positions[:, None] + slot_index[None, :]).reshape(total_row_count).astype(jnp.float32)
    )
    query_rows = rotate(head_norm(query_raw, q_gain), position).astype(jnp.bfloat16)
    query_rows = query_rows.reshape(
        stream_list, cache_slot_count, KEY_VALUE_HEADS, query_group_size, HEAD_SIZE
    )
    fresh_keys = rotate(head_norm(unnormed_key, k_gain), position).astype(jnp.bfloat16)
    fresh_keys = fresh_keys.reshape(stream_list, cache_slot_count, KEY_VALUE_HEADS, HEAD_SIZE)
    earlier_keys = stored_keys.reshape(stream_list, cache_frame_count, KEY_VALUE_HEADS, HEAD_SIZE)
    earlier_values = stored_values.reshape(
        stream_list, cache_frame_count, KEY_VALUE_HEADS, HEAD_SIZE
    )
    score_scale = 1.0 / math.sqrt(HEAD_SIZE)
    old_scores = (
        jnp.einsum(
            "sckgd,sfkd->skgcf", query_rows, earlier_keys, preferred_element_type=jnp.float32
        )
        * score_scale
    )
    new_scores = (
        jnp.einsum("sckgd,sjkd->skgcj", query_rows, fresh_keys, preferred_element_type=jnp.float32)
        * score_scale
    )
    frame_index = jnp.arange(cache_frame_count, dtype=jnp.int32)
    old_live = (frame_index[None, :] < fill_positions[:, None])[:, None, None, None, :]
    new_live = (slot_index[None, None, :] <= slot_index[None, :, None]) & (
        slot_index[None, None, :] < span_lengths[:, None, None]
    )
    new_live = new_live[:, None, None, :, :]
    old_scores = jnp.where(old_live, old_scores, -1e30)
    new_scores = jnp.where(new_live, new_scores, -1e30)
    row_max = jnp.maximum(
        jnp.max(old_scores, axis=-1, keepdims=True), jnp.max(new_scores, axis=-1, keepdims=True)
    )
    old_weights = jnp.exp(old_scores - row_max)
    new_weights = jnp.exp(new_scores - row_max)
    denominator = jnp.sum(old_weights, axis=-1) + jnp.sum(new_weights, axis=-1)
    mixed_heads = jnp.einsum(
        "skgcf,sfkd->sckgd",
        old_weights.astype(jnp.bfloat16),
        earlier_values,
        preferred_element_type=jnp.float32,
    )
    mixed_heads = mixed_heads + jnp.einsum(
        "skgcj,sjkd->sckgd",
        new_weights.astype(jnp.bfloat16),
        fresh_values,
        preferred_element_type=jnp.float32,
    )
    mixed_heads = mixed_heads / jnp.transpose(denominator, (0, 3, 1, 2))[..., None]
    query_live = (slot_index[None, :] < span_lengths[:, None])[:, :, None, None, None]
    mixed_heads = jnp.where(query_live, mixed_heads, 0.0)
    return mixed_heads.reshape(total_row_count, QUERY_HEADS * HEAD_SIZE).astype(jnp.bfloat16)


def shards(
    tokens,
    ln_gain,
    w_qkv,
    q_gain,
    k_gain,
    stored_keys,
    stored_values,
    span_lengths,
    fill_positions,
    w_out,
):
    wide_count = lax.axis_size("wide")
    own_rows = lax.all_to_all(tokens, "narrow", split_axis=0, concat_axis=1, tiled=True)
    token_values = own_rows.astype(jnp.float32)
    own_squares = jnp.sum(token_values * token_values, axis=1)
    normed = (token_values * ln_gain[None, :]).astype(jnp.bfloat16)
    every_normed = lax.all_gather(normed, "wide", axis=0, tiled=True)
    columns = lax.all_gather(w_qkv, "narrow", axis=0, tiled=True)
    projected = jnp.dot(every_normed, columns, preferred_element_type=jnp.float32)
    packed = lax.all_to_all(
        projected.astype(jnp.bfloat16), "wide", split_axis=0, concat_axis=1, tiled=True
    )
    attended = attend(
        packed,
        own_squares,
        wide_count,
        q_gain,
        k_gain,
        stored_keys,
        stored_values,
        span_lengths,
        fill_positions,
    )
    every_row = lax.all_gather(attended, "narrow", axis=0, tiled=True)
    result = jnp.dot(
        every_row,
        lax.all_gather(w_out, "wide", axis=0, tiled=True),
        preferred_element_type=jnp.float32,
    )
    return result.astype(jnp.bfloat16)


def solution(mesh):
    placed = (
        P("wide", "narrow"),
        P(),
        P("narrow", "wide"),
        P(),
        P(),
        P(("wide", "narrow"), None, None),
        P(("wide", "narrow"), None, None),
        P(("wide", "narrow")),
        P(("wide", "narrow")),
        P("wide", "narrow"),
    )
    return jax.shard_map(
        shards, mesh=mesh, in_specs=placed, out_specs=P("wide", "narrow"), check_vma=False
    )
```

```python
import math

import jax
import jax.numpy as jnp
from jax import lax
from jax.sharding import PartitionSpec as P

D = 5120
QUERY_HEADS = 64
KEY_VALUE_HEADS = 8
HEAD_SIZE = 128


EPSILON = 1e-06
ROPE_BASE = 1000000.0


def head_norm(vectors, gains):
    mean_square = jnp.mean(vectors * vectors, axis=-1, keepdims=True)
    return vectors * lax.rsqrt(mean_square + EPSILON) * gains


def rotate(vectors, position):
    half_dim = vectors.shape[-1] // 2
    frequency = jnp.exp(
        jnp.arange(half_dim, dtype=jnp.float32) * (-2.0 * math.log(ROPE_BASE) / vectors.shape[-1])
    )
    angles = position[:, None] * frequency[None, :]
    cosine = jnp.cos(angles)[:, None, :]
    sine_part = jnp.sin(angles)[:, None, :]
    first_half = vectors[..., :half_dim]
    second_half = vectors[..., half_dim:]
    return jnp.concatenate(
        [
            first_half * cosine - second_half * sine_part,
            second_half * cosine + first_half * sine_part,
        ],
        axis=-1,
    )


def attend(
    packed,
    own_squares,
    head_groups,
    q_gain,
    k_gain,
    stored_keys,
    stored_values,
    span_lengths,
    fill_positions,
):
    stream_list = span_lengths.shape[0]
    total_row_count = packed.shape[0]
    cache_slot_count = total_row_count // stream_list
    cache_frame_count = stored_keys.shape[1]
    query_group_size = QUERY_HEADS // KEY_VALUE_HEADS
    query_columns = QUERY_HEADS * HEAD_SIZE // head_groups
    key_columns = KEY_VALUE_HEADS * HEAD_SIZE // head_groups
    grouped_queries = packed.reshape(total_row_count, head_groups, query_columns + 2 * key_columns)
    query_raw = (
        grouped_queries[:, :, :query_columns]
        .reshape(total_row_count, QUERY_HEADS, HEAD_SIZE)
        .astype(jnp.float32)
    )
    unnormed_key = (
        grouped_queries[:, :, query_columns : query_columns + key_columns]
        .reshape(total_row_count, KEY_VALUE_HEADS, HEAD_SIZE)
        .astype(jnp.float32)
    )
    unnormed_value = (
        grouped_queries[:, :, query_columns + key_columns :]
        .reshape(total_row_count, KEY_VALUE_HEADS * HEAD_SIZE)
        .astype(jnp.float32)
    )
    inverse_root_mean = lax.rsqrt(own_squares / D + EPSILON)
    fresh_values = (
        (unnormed_value * inverse_root_mean[:, None])
        .astype(jnp.bfloat16)
        .reshape(stream_list, cache_slot_count, KEY_VALUE_HEADS, HEAD_SIZE)
    )
    slot_index = jnp.arange(cache_slot_count, dtype=jnp.int32)
    position = (
        (fill_positions[:, None] + slot_index[None, :]).reshape(total_row_count).astype(jnp.float32)
    )
    query_rows = rotate(head_norm(query_raw, q_gain), position).astype(jnp.bfloat16)
    query_rows = query_rows.reshape(
        stream_list, cache_slot_count, KEY_VALUE_HEADS, query_group_size, HEAD_SIZE
    )
    fresh_keys = rotate(head_norm(unnormed_key, k_gain), position).astype(jnp.bfloat16)
    fresh_keys = fresh_keys.reshape(stream_list, cache_slot_count, KEY_VALUE_HEADS, HEAD_SIZE)
    earlier_keys = stored_keys.reshape(stream_list, cache_frame_count, KEY_VALUE_HEADS, HEAD_SIZE)
    earlier_values = stored_values.reshape(
        stream_list, cache_frame_count, KEY_VALUE_HEADS, HEAD_SIZE
    )
    score_scale = 1.0 / math.sqrt(HEAD_SIZE)
    old_scores = (
        jnp.einsum(
            "sckgd,sfkd->skgcf", query_rows, earlier_keys, preferred_element_type=jnp.float32
        )
        * score_scale
    )
    new_scores = (
        jnp.einsum("sckgd,sjkd->skgcj", query_rows, fresh_keys, preferred_element_type=jnp.float32)
        * score_scale
    )
    frame_index = jnp.arange(cache_frame_count, dtype=jnp.int32)
    old_live = (frame_index[None, :] < fill_positions[:, None])[:, None, None, None, :]
    new_live = (slot_index[None, None, :] <= slot_index[None, :, None]) & (
        slot_index[None, None, :] < span_lengths[:, None, None]
    )
    new_live = new_live[:, None, None, :, :]
    old_scores = jnp.where(old_live, old_scores, -1e30)
    new_scores = jnp.where(new_live, new_scores, -1e30)
    row_max = jnp.maximum(
        jnp.max(old_scores, axis=-1, keepdims=True), jnp.max(new_scores, axis=-1, keepdims=True)
    )
    old_weights = jnp.exp(old_scores - row_max)
    new_weights = jnp.exp(new_scores - row_max)
    denominator = jnp.sum(old_weights, axis=-1) + jnp.sum(new_weights, axis=-1)
    mixed_heads = jnp.einsum(
        "skgcf,sfkd->sckgd",
        old_weights.astype(jnp.bfloat16),
        earlier_values,
        preferred_element_type=jnp.float32,
    )
    mixed_heads = mixed_heads + jnp.einsum(
        "skgcj,sjkd->sckgd",
        new_weights.astype(jnp.bfloat16),
        fresh_values,
        preferred_element_type=jnp.float32,
    )
    mixed_heads = mixed_heads / jnp.transpose(denominator, (0, 3, 1, 2))[..., None]
    query_live = (slot_index[None, :] < span_lengths[:, None])[:, :, None, None, None]
    mixed_heads = jnp.where(query_live, mixed_heads, 0.0)
    return mixed_heads.reshape(total_row_count, QUERY_HEADS * HEAD_SIZE).astype(jnp.bfloat16)


def place(buffer, block, *index):
    start = tuple(index) + (0,) * (buffer.ndim - len(index))
    shape = (1,) * (buffer.ndim - block.ndim) + block.shape
    return lax.dynamic_update_slice(buffer, block.reshape(shape), start)


def gather_pairs_and_ring(block, axis, ring, pair, rest):
    count = lax.axis_size(axis)
    coordinates = [(ring(i), pair(i), rest(i)) for i in range(count)]
    index_of = {c: i for i, c in enumerate(coordinates)}

    def moved(steps, flip):
        return [
            (i, index_of[((r + steps) % 4, p ^ flip, q)]) for i, (r, p, q) in enumerate(coordinates)
        ]

    swap, up, down = moved(0, 1), moved(1, 0), moved(-1, 0)
    me = lax.axis_index(axis)
    at_ring, at_pair = ring(me), pair(me)
    half = block.shape[0] // 2
    full = jnp.zeros((4, 2, 2, half) + block.shape[1:], block.dtype)

    def halves(b):
        return b.reshape((2, half) + block.shape[1:])

    def spread(full, own, at_pair, from_up, from_down, far_up, far_down):
        full = place(full, halves(own), at_ring, at_pair)
        full = place(full, halves(from_up), (at_ring + 3) % 4, at_pair)
        full = place(full, halves(from_down), (at_ring + 1) % 4, at_pair)
        full = place(full, far_up, (at_ring + 2) % 4, at_pair, 0)
        full = place(full, far_down, (at_ring + 2) % 4, at_pair, 1)
        return full

    from_up = lax.ppermute(block, axis, up)
    from_down = lax.ppermute(block, axis, down)
    swapped = lax.ppermute(block, axis, swap)
    far_up = lax.ppermute(from_up[:half], axis, up)
    far_down = lax.ppermute(from_down[half:], axis, down)
    swapped_up = lax.ppermute(swapped, axis, up)
    swapped_down = lax.ppermute(swapped, axis, down)
    swapped_far_up = lax.ppermute(swapped_up[:half], axis, up)
    swapped_far_down = lax.ppermute(swapped_down[half:], axis, down)
    full = spread(full, block, at_pair, from_up, from_down, far_up, far_down)
    full = spread(
        full, swapped, 1 - at_pair, swapped_up, swapped_down, swapped_far_up, swapped_far_down
    )
    return full.reshape((4, 2) + block.shape)


def gather_narrow(block):
    full = gather_pairs_and_ring(block, "narrow", lambda i: i // 2, lambda i: i % 2, lambda i: 0)
    return full.reshape((8 * block.shape[0],) + block.shape[1:])


def gather_wide(block):
    full = gather_pairs_and_ring(
        block, "wide", lambda i: i // 2 % 4, lambda i: i // 8, lambda i: i % 2
    )
    full = jnp.transpose(full, (1, 0) + tuple(range(2, full.ndim)))
    other = lax.ppermute(full, "wide", [(i, i ^ 1) for i in range(16)])
    core = lax.axis_index("wide") % 2
    both = jnp.where(core == 0, jnp.stack([full, other], 2), jnp.stack([other, full], 2))
    return both.reshape((16 * block.shape[0],) + block.shape[1:])


def shards(
    tokens,
    ln_gain,
    w_qkv,
    q_gain,
    k_gain,
    stored_keys,
    stored_values,
    span_lengths,
    fill_positions,
    w_out,
):
    wide_count = lax.axis_size("wide")
    own_rows = lax.all_to_all(tokens, "narrow", split_axis=0, concat_axis=1, tiled=True)
    token_values = own_rows.astype(jnp.float32)
    own_squares = jnp.sum(token_values * token_values, axis=1)
    normed = (token_values * ln_gain[None, :]).astype(jnp.bfloat16)
    every_normed = gather_wide(normed)
    columns = gather_narrow(w_qkv)
    projected = jnp.dot(every_normed, columns, preferred_element_type=jnp.float32)
    projected, w_out = lax.optimization_barrier((projected.astype(jnp.bfloat16), w_out))
    every_w_out = lax.all_gather(w_out, "wide", axis=0, tiled=True)
    packed = lax.all_to_all(
        projected, "wide", split_axis=0, concat_axis=1, tiled=True
    )
    attended = attend(
        packed,
        own_squares,
        wide_count,
        q_gain,
        k_gain,
        stored_keys,
        stored_values,
        span_lengths,
        fill_positions,
    )
    every_row = gather_narrow(attended)
    result = jnp.dot(
        every_row,
        every_w_out,
        preferred_element_type=jnp.float32,
    )
    return result.astype(jnp.bfloat16)


def solution(mesh):
    placed = (
        P("wide", "narrow"),
        P(),
        P("narrow", "wide"),
        P(),
        P(),
        P(("wide", "narrow"), None, None),
        P(("wide", "narrow"), None, None),
        P(("wide", "narrow")),
        P(("wide", "narrow")),
        P("wide", "narrow"),
    )
    return jax.shard_map(
        shards, mesh=mesh, in_specs=placed, out_specs=P("wide", "narrow"), check_vma=False
    )
```

```python
import math

import jax
import jax.numpy as jnp
from jax import lax
from jax.experimental import pallas as pl
from jax.experimental.pallas import tpu as pltpu
from jax.sharding import PartitionSpec as P

D = 5120
QUERY_HEADS = 64
KEY_VALUE_HEADS = 8
HEAD_SIZE = 128


EPSILON = 1e-06
ROPE_BASE = 1000000.0


def turn_tables(fill_positions, slots):
    half = HEAD_SIZE // 2
    slot_index = jnp.arange(slots, dtype=jnp.int32)
    position = (fill_positions[:, None] + slot_index[None, :]).reshape(-1).astype(jnp.float32)
    frequency = jnp.exp(
        jnp.arange(half, dtype=jnp.float32) * (-2.0 * math.log(ROPE_BASE) / HEAD_SIZE)
    )
    angles = position[:, None] * frequency[None, :]
    cosine, sine = jnp.cos(angles), jnp.sin(angles)
    return (
        jnp.concatenate([cosine, cosine], axis=1),
        jnp.concatenate([-sine, sine], axis=1),
    )


def attend_kernel(
    fills,
    spans,
    packed,
    inverse,
    cosine,
    sine,
    q_gain,
    k_gain,
    keys,
    values,
    attended,
):
    stream = pl.program_id(0)
    fill, span = fills[stream], spans[stream]
    slots = packed.shape[1]
    frames = keys.shape[1]
    group = QUERY_HEADS // KEY_VALUE_HEADS
    rows = group * slots
    cos_one, sin_one = cosine[...], sine[...]

    def turned(vectors, gains, cos_rows, sin_rows):
        mean_square = jnp.mean(vectors * vectors, axis=-1, keepdims=True)
        normed = vectors * lax.rsqrt(mean_square + EPSILON) * gains
        swapped = pltpu.roll(normed, HEAD_SIZE // 2, 1)
        return (normed * cos_rows + swapped * sin_rows).astype(jnp.bfloat16)

    cos_all = jnp.concatenate([cos_one] * group, axis=0)
    sin_all = jnp.concatenate([sin_one] * group, axis=0)
    low = lax.broadcasted_iota(jnp.int32, (slots, HEAD_SIZE), 1) < HEAD_SIZE // 2
    frame_live = lax.broadcasted_iota(jnp.int32, (rows, frames), 1) < fill
    slot_row = lax.broadcasted_iota(jnp.int32, (group, slots, slots), 1).reshape(rows, slots)
    slot_column = lax.broadcasted_iota(jnp.int32, (rows, slots), 1)
    slot_live = (slot_column <= slot_row) & (slot_column < span)
    row_live = (
        lax.broadcasted_iota(jnp.int32, (group, slots, HEAD_SIZE), 1).reshape(rows, HEAD_SIZE)
        < span
    )
    query_columns = group // 2 * HEAD_SIZE
    contract_last = (((1,), (1,)), ((), ()))
    score_scale = 1.0 / math.sqrt(HEAD_SIZE)
    for head in range(KEY_VALUE_HEADS):
        queries = jnp.concatenate(
            [
                packed[2 * head + g // 4, :, g % 4 * HEAD_SIZE : (g % 4 + 1) * HEAD_SIZE]
                for g in range(group)
            ],
            axis=0,
        ).astype(jnp.float32)
        queries = turned(queries, q_gain[...], cos_all, sin_all)
        first = packed[2 * head, :, query_columns:].astype(jnp.float32)
        second = packed[2 * head + 1, :, query_columns:].astype(jnp.float32)
        fresh_key = jnp.where(low, first, pltpu.roll(second, HEAD_SIZE // 2, 1))
        fresh_value = jnp.where(low, pltpu.roll(first, HEAD_SIZE // 2, 1), second)
        fresh_key = turned(fresh_key, k_gain[...], cos_one, sin_one)
        fresh_value = (fresh_value * inverse[...]).astype(jnp.bfloat16)
        columns = slice(head * HEAD_SIZE, (head + 1) * HEAD_SIZE)
        old = lax.dot_general(
            queries, keys[0, :, columns], contract_last, preferred_element_type=jnp.float32
        )
        new = lax.dot_general(
            queries, fresh_key, contract_last, preferred_element_type=jnp.float32
        )
        old = jnp.where(frame_live, old * score_scale, -1e30)
        new = jnp.where(slot_live, new * score_scale, -1e30)
        top = jnp.maximum(
            jnp.max(old, axis=-1, keepdims=True), jnp.max(new, axis=-1, keepdims=True)
        )
        old, new = jnp.exp(old - top), jnp.exp(new - top)
        total = jnp.sum(old, axis=-1, keepdims=True) + jnp.sum(new, axis=-1, keepdims=True)
        mixed = jnp.dot(
            old.astype(jnp.bfloat16), values[0, :, columns], preferred_element_type=jnp.float32
        ) + jnp.dot(new.astype(jnp.bfloat16), fresh_value, preferred_element_type=jnp.float32)
        mixed = jnp.where(row_live, mixed / total, 0.0).astype(jnp.bfloat16)
        for g in range(group):
            start = (head * group + g) * HEAD_SIZE
            attended[:, start : start + HEAD_SIZE] = mixed[g * slots : (g + 1) * slots]


def attend(packed, inverse, cosine, sine, q_gain, k_gain, keys, values, spans, fills, first=0):
    groups, rows, columns = packed.shape
    slots = 16
    streams = rows // slots
    frames, width = keys.shape[1:]
    tables = pl.BlockSpec((slots, HEAD_SIZE), lambda s, *_: (s, 0))
    gains = pl.BlockSpec((1, HEAD_SIZE), lambda s, *_: (0, 0))
    cache = pl.BlockSpec((1, frames, width), lambda s, *_: (first + s, 0, 0))
    return pl.pallas_call(
        attend_kernel,
        grid_spec=pltpu.PrefetchScalarGridSpec(
            num_scalar_prefetch=2,
            grid=(streams,),
            in_specs=[
                pl.BlockSpec((groups, slots, columns), lambda s, *_: (0, s, 0)),
                tables,
                tables,
                tables,
                gains,
                gains,
                cache,
                cache,
            ],
            out_specs=pl.BlockSpec((slots, QUERY_HEADS * HEAD_SIZE), lambda s, *_: (s, 0)),
        ),
        out_shape=jax.ShapeDtypeStruct((rows, QUERY_HEADS * HEAD_SIZE), jnp.bfloat16),
        compiler_params=pltpu.CompilerParams(vmem_limit_bytes=32 * 1024 * 1024),
        cost_estimate=pl.CostEstimate(
            flops=4 * rows * QUERY_HEADS * HEAD_SIZE * (frames + slots),
            bytes_accessed=4 * streams * frames * width + 4 * rows * 9216,
            transcendentals=rows * QUERY_HEADS * (frames + slots),
        ),
        name="attend",
    )(
        fills[first : first + streams],
        spans[first : first + streams],
        packed,
        inverse,
        cosine,
        sine,
        q_gain[None],
        k_gain[None],
        keys,
        values,
    )


class Ring:
    def __init__(self, axis):
        self.axis = axis
        if axis == "narrow":
            self.split = lambda i: (i // 2, i % 2, 0)
        else:
            self.split = lambda i: (i // 2 % 4, i // 8, i % 2)
        self.places = [self.split(i) for i in range(lax.axis_size(axis))]
        index_of = {place: i for i, place in enumerate(self.places)}

        def pairs(steps, flip, core):
            return [
                (i, index_of[((r + steps) % 4, p ^ flip, c ^ core)])
                for i, (r, p, c) in enumerate(self.places)
            ]

        self.pairs = pairs
        self.at_ring, self.at_pair, self.at_core = self.split(lax.axis_index(axis))

    def up(self, block):
        return lax.ppermute(block, self.axis, self.pairs(1, 0, 0))

    def down(self, block):
        return lax.ppermute(block, self.axis, self.pairs(-1, 0, 0))

    def swap(self, block):
        return lax.ppermute(block, self.axis, self.pairs(0, 1, 0))

    def cores(self, block):
        return lax.ppermute(block, self.axis, self.pairs(0, 0, 1))

    def ring(self, steps):
        return (self.at_ring + steps) % 4


def place(buffer, block, *index):
    start = tuple(index) + (0,) * (buffer.ndim - len(index))
    shape = (1,) * (buffer.ndim - block.ndim) + block.shape
    return lax.dynamic_update_slice(buffer, block.reshape(shape), start)


def halves(block):
    return block.reshape((2, -1) + block.shape[1:])


def gathered_wide(wide, own_core, other_core):
    block = own_core[0]
    rows, half = block.shape[0], block.shape[0] // 2
    every = jnp.zeros((2, 4, 2, 2, half) + block.shape[1:], block.dtype)
    one, other = wide.at_pair, 1 - wide.at_pair
    for core, pieces in ((wide.at_core, own_core), (1 - wide.at_core, other_core)):
        own, up, down, swap, two_up, two_down, far_up, far_down = pieces
        every = place(every, halves(own), one, wide.ring(0), core)
        every = place(every, halves(up), one, wide.ring(3), core)
        every = place(every, halves(down), one, wide.ring(1), core)
        every = place(every, halves(swap), other, wide.ring(0), core)
        every = place(every, halves(two_up[:rows]), other, wide.ring(3), core)
        every = place(every, halves(two_down[:rows]), other, wide.ring(1), core)
        every = place(every, two_up[rows:], one, wide.ring(2), core, 0)
        every = place(every, two_down[rows:], one, wide.ring(2), core, 1)
        every = place(every, far_up, other, wide.ring(2), core, 0)
        every = place(every, far_down, other, wide.ring(2), core, 1)
    return every.reshape((-1,) + block.shape[1:])


def shards(
    tokens,
    ln_gain,
    w_qkv,
    q_gain,
    k_gain,
    stored_keys,
    stored_values,
    span_lengths,
    fill_positions,
    w_out,
):
    barrier = lax.optimization_barrier
    wide, narrow = Ring("wide"), Ring("narrow")
    wide_count = lax.axis_size("wide")
    streams = span_lengths.shape[0]
    rows = tokens.shape[0] // lax.axis_size("narrow")
    slots = rows // streams
    depth = w_qkv.shape[0]
    half_rows, half_depth = rows // 2, depth // 2

    own_rows = lax.all_to_all(tokens, "narrow", split_axis=0, concat_axis=1, tiled=True)
    w_swap = narrow.swap(w_qkv)
    token_values = own_rows.astype(jnp.float32)
    own_squares = jnp.sum(token_values * token_values, axis=1)
    normed = (token_values * ln_gain[None, :]).astype(jnp.bfloat16)
    w_qkv, w_swap, normed = barrier((w_qkv, w_swap, normed))

    w_up, w_down = narrow.up(w_qkv), narrow.down(w_qkv)
    t_up, t_down, t_swap = wide.up(normed), wide.down(normed), wide.swap(normed)
    w_up, w_down, t_up, t_down, t_swap = barrier((w_up, w_down, t_up, t_down, t_swap))

    w_two_up = narrow.up(jnp.concatenate([w_swap, w_up[:half_depth]]))
    w_two_down = narrow.down(jnp.concatenate([w_swap, w_down[half_depth:]]))
    t_two_up = wide.up(jnp.concatenate([t_swap, t_up[:half_rows]]))
    t_two_down = wide.down(jnp.concatenate([t_swap, t_down[half_rows:]]))
    near = wide.cores(jnp.stack([normed, t_up, t_down, t_swap]))
    t_two_up, t_two_down, w_two_up, w_two_down, near = barrier(
        (t_two_up, t_two_down, w_two_up, w_two_down, near)
    )

    w_far_up = narrow.up(w_two_up[:half_depth])
    w_far_down = narrow.down(w_two_down[half_depth:depth])
    t_far_up = wide.up(t_two_up[:half_rows])
    t_far_down = wide.down(t_two_down[half_rows:rows])
    two = wide.cores(jnp.stack([t_two_up, t_two_down]))
    far = wide.cores(jnp.stack([t_far_up, t_far_down]))

    columns = jnp.zeros((4, 2, 2, half_depth) + w_qkv.shape[1:], w_qkv.dtype)
    one, other = narrow.at_pair, 1 - narrow.at_pair
    columns = place(columns, halves(w_qkv), narrow.ring(0), one)
    columns = place(columns, halves(w_up), narrow.ring(3), one)
    columns = place(columns, halves(w_down), narrow.ring(1), one)
    columns = place(columns, halves(w_swap), narrow.ring(0), other)
    columns = place(columns, halves(w_two_up[:depth]), narrow.ring(3), other)
    columns = place(columns, halves(w_two_down[:depth]), narrow.ring(1), other)
    columns = place(columns, w_two_up[depth:], narrow.ring(2), one, 0)
    columns = place(columns, w_two_down[depth:], narrow.ring(2), one, 1)
    columns = place(columns, w_far_up, narrow.ring(2), other, 0)
    columns = place(columns, w_far_down, narrow.ring(2), other, 1)
    columns = columns.reshape(-1, w_qkv.shape[1])

    every = gathered_wide(
        wide,
        (normed, t_up, t_down, t_swap, t_two_up, t_two_down, t_far_up, t_far_down),
        (*near, *two, *far),
    )

    every, w_out = barrier((every, w_out))
    o_up, o_down, o_swap = wide.up(w_out), wide.down(w_out), wide.swap(w_out)
    projected = jnp.dot(every, columns, preferred_element_type=jnp.float32).astype(jnp.bfloat16)
    packed = lax.all_to_all(
        projected.reshape(wide_count, rows, -1), "wide", split_axis=0, concat_axis=0, tiled=True
    )
    packed, o_up, o_down, o_swap = barrier((packed, o_up, o_down, o_swap))
    half_out, out_rows = w_out.shape[0] // 2, w_out.shape[0]
    o_two_up = wide.up(jnp.concatenate([o_swap, o_up[:half_out]]))
    o_two_down = wide.down(jnp.concatenate([o_swap, o_down[half_out:]]))
    inverse = jnp.broadcast_to(lax.rsqrt(own_squares / D + EPSILON)[:, None], (rows, HEAD_SIZE))
    cosine, sine = turn_tables(fill_positions, slots)
    attended = attend(
        packed,
        inverse,
        cosine,
        sine,
        q_gain,
        k_gain,
        stored_keys,
        stored_values,
        span_lengths,
        fill_positions,
    )

    quarter = rows // 4
    attended, o_two_up, o_two_down = barrier((attended, o_two_up, o_two_down))
    a_up, a_down, a_swap = narrow.up(attended), narrow.down(attended), narrow.swap(attended)
    o_far_up = wide.up(o_two_up[:half_out])
    o_far_down = wide.down(o_two_down[half_out:out_rows])
    a_up, a_down, a_swap, o_far_up, o_far_down = barrier(
        (a_up, a_down, a_swap, o_far_up, o_far_down)
    )
    b_up = narrow.up(jnp.concatenate([a_swap[half_rows:], a_up[:half_rows]]))
    b_down = narrow.down(jnp.concatenate([a_swap[half_rows:], a_down[half_rows:]]))
    b_swap = narrow.swap(jnp.concatenate([a_up[:half_rows], a_down[:half_rows]]))
    o_near = wide.cores(jnp.stack([w_out, o_up, o_down, o_swap]))
    o_two = wide.cores(jnp.stack([o_two_up, o_two_down]))
    o_far = wide.cores(jnp.stack([o_far_up, o_far_down]))
    b_up, b_down, b_swap, o_near, o_two, o_far = barrier(
        (b_up, b_down, b_swap, o_near, o_two, o_far)
    )
    c_up = narrow.up(b_up[:quarter])
    c_down = narrow.down(b_down[quarter:half_rows])
    c_swap = narrow.swap(b_up[half_rows:])
    every_w_out = gathered_wide(
        wide,
        (w_out, o_up, o_down, o_swap, o_two_up, o_two_down, o_far_up, o_far_down),
        (*o_near, *o_two, *o_far),
    )

    most = jnp.concatenate(
        [
            attended,
            a_swap,
            a_up,
            b_swap[:half_rows],
            b_up[:half_rows],
            a_down,
            b_swap[half_rows:],
            b_down[:half_rows],
            b_up[half_rows:],
            b_down[half_rows:],
        ]
    )
    last = jnp.concatenate([c_swap, c_up, c_down])
    project = lambda b: jnp.dot(b, every_w_out, preferred_element_type=jnp.float32).astype(
        jnp.bfloat16
    )
    most = project(most)
    result = jnp.zeros((4, 2, rows, most.shape[1]), most.dtype)
    one, other = narrow.at_pair, 1 - narrow.at_pair
    for i, (steps, pair) in enumerate(
        ((0, one), (0, other), (3, one), (3, other), (1, one), (1, other), (2, one))
    ):
        result = place(result, most[i * rows : (i + 1) * rows], narrow.ring(steps), pair)
    result = place(result, project(last), narrow.ring(2), other)
    return result.reshape(-1, most.shape[1])


def solution(mesh):
    placed = (
        P("wide", "narrow"),
        P(),
        P("narrow", "wide"),
        P(),
        P(),
        P(("wide", "narrow"), None, None),
        P(("wide", "narrow"), None, None),
        P(("wide", "narrow")),
        P(("wide", "narrow")),
        P("wide", "narrow"),
    )
    return jax.shard_map(
        shards, mesh=mesh, in_specs=placed, out_specs=P("wide", "narrow"), check_vma=False
    )
```

```python
import functools
import math

import jax
import jax.numpy as jnp
from jax import lax
from jax.experimental import pallas as pl
from jax.experimental.pallas import tpu as pltpu
from jax.sharding import PartitionSpec as P

D = 5120
QUERY_HEADS = 64
KEY_VALUE_HEADS = 8
HEAD_SIZE = 128


EPSILON = 1e-06
ROPE_BASE = 1000000.0


def turn_tables(fill_positions, slots):
    half = HEAD_SIZE // 2
    slot_index = jnp.arange(slots, dtype=jnp.int32)
    position = (fill_positions[:, None] + slot_index[None, :]).reshape(-1).astype(jnp.float32)
    frequency = jnp.exp(
        jnp.arange(half, dtype=jnp.float32) * (-2.0 * math.log(ROPE_BASE) / HEAD_SIZE)
    )
    angles = position[:, None] * frequency[None, :]
    cosine, sine = jnp.cos(angles), jnp.sin(angles)
    return (
        jnp.concatenate([cosine, cosine], axis=1),
        jnp.concatenate([-sine, sine], axis=1),
    )


def attend_kernel(
    fills,
    spans,
    packed,
    inverse,
    cosine,
    sine,
    q_gain,
    k_gain,
    keys,
    values,
    attended,
):
    stream = pl.program_id(0)
    fill, span = fills[stream], spans[stream]
    slots = packed.shape[1]
    frames = keys.shape[1]
    group = QUERY_HEADS // KEY_VALUE_HEADS
    rows = group * slots
    cos_one, sin_one = cosine[...], sine[...]

    def turned(vectors, gains, cos_rows, sin_rows):
        mean_square = jnp.mean(vectors * vectors, axis=-1, keepdims=True)
        normed = vectors * lax.rsqrt(mean_square + EPSILON) * gains
        swapped = pltpu.roll(normed, HEAD_SIZE // 2, 1)
        return (normed * cos_rows + swapped * sin_rows).astype(jnp.bfloat16)

    cos_all = jnp.concatenate([cos_one] * group, axis=0)
    sin_all = jnp.concatenate([sin_one] * group, axis=0)
    low = lax.broadcasted_iota(jnp.int32, (slots, HEAD_SIZE), 1) < HEAD_SIZE // 2
    frame_live = lax.broadcasted_iota(jnp.int32, (rows, frames), 1) < fill
    slot_row = lax.broadcasted_iota(jnp.int32, (group, slots, HEAD_SIZE), 1)
    slot_row = slot_row.reshape(rows, HEAD_SIZE)
    slot_column = lax.broadcasted_iota(jnp.int32, (rows, HEAD_SIZE), 1)
    slot_live = (slot_column <= slot_row) & (slot_column < span)
    row_live = slot_row < span
    empty = jnp.zeros((HEAD_SIZE - slots, HEAD_SIZE), jnp.bfloat16)
    query_columns = group // 2 * HEAD_SIZE
    contract_last = (((1,), (1,)), ((), ()))
    score_scale = 1.0 / math.sqrt(HEAD_SIZE)
    for head in range(KEY_VALUE_HEADS):
        queries = jnp.concatenate(
            [
                packed[2 * head + g // 4, :, g % 4 * HEAD_SIZE : (g % 4 + 1) * HEAD_SIZE]
                for g in range(group)
            ],
            axis=0,
        ).astype(jnp.float32)
        queries = turned(queries, q_gain[...], cos_all, sin_all)
        first = packed[2 * head, :, query_columns:].astype(jnp.float32)
        second = packed[2 * head + 1, :, query_columns:].astype(jnp.float32)
        fresh_key = jnp.where(low, first, pltpu.roll(second, HEAD_SIZE // 2, 1))
        fresh_value = jnp.where(low, pltpu.roll(first, HEAD_SIZE // 2, 1), second)
        fresh_key = jnp.concatenate([turned(fresh_key, k_gain[...], cos_one, sin_one), empty])
        fresh_value = jnp.concatenate([(fresh_value * inverse[...]).astype(jnp.bfloat16), empty])
        columns = slice(head * HEAD_SIZE, (head + 1) * HEAD_SIZE)
        old = lax.dot_general(
            queries, keys[0, :, columns], contract_last, preferred_element_type=jnp.float32
        )
        new = lax.dot_general(
            queries, fresh_key, contract_last, preferred_element_type=jnp.float32
        )
        old = jnp.where(frame_live, old * score_scale, -1e30)
        new = jnp.where(slot_live, new * score_scale, -1e30)
        scores = jnp.concatenate([old, new], axis=1)
        weights = jnp.exp(scores - jnp.max(scores, axis=-1, keepdims=True))
        total = jnp.sum(weights, axis=-1, keepdims=True)
        weights = weights.astype(jnp.bfloat16)
        mixed = jnp.dot(
            weights[:, :frames], values[0, :, columns], preferred_element_type=jnp.float32
        ) + jnp.dot(weights[:, frames:], fresh_value, preferred_element_type=jnp.float32)
        mixed = jnp.where(row_live, mixed / total, 0.0).astype(jnp.bfloat16)
        for g in range(group):
            start = (head * group + g) * HEAD_SIZE
            attended[:, start : start + HEAD_SIZE] = mixed[g * slots : (g + 1) * slots]


def attend(packed, inverse, cosine, sine, q_gain, k_gain, keys, values, spans, fills):
    groups, rows, columns = packed.shape
    streams, frames, width = keys.shape
    slots = rows // streams
    heads = QUERY_HEADS * HEAD_SIZE
    tables = pl.BlockSpec((slots, HEAD_SIZE), lambda s, *_: (s, 0))
    gains = pl.BlockSpec((1, HEAD_SIZE), lambda s, *_: (0, 0))
    cache = pl.BlockSpec((1, frames, width), lambda s, *_: (s, 0, 0))
    return pl.pallas_call(
        attend_kernel,
        grid_spec=pltpu.PrefetchScalarGridSpec(
            num_scalar_prefetch=2,
            grid=(streams,),
            in_specs=[
                pl.BlockSpec((groups, slots, columns), lambda s, *_: (0, s, 0)),
                tables,
                tables,
                tables,
                gains,
                gains,
                cache,
                cache,
            ],
            out_specs=pl.BlockSpec((slots, heads), lambda s, *_: (s, 0)),
        ),
        out_shape=jax.ShapeDtypeStruct((rows, heads), jnp.bfloat16),
        compiler_params=pltpu.CompilerParams(vmem_limit_bytes=24 << 20),
        cost_estimate=pl.CostEstimate(
            flops=4 * rows * heads * (frames + slots),
            bytes_accessed=4 * streams * frames * width + 4 * rows * 9216,
            transcendentals=rows * QUERY_HEADS * (frames + slots),
        ),
        name="attend",
    )(
        fills,
        spans,
        packed,
        inverse,
        cosine,
        sine,
        q_gain[None],
        k_gain[None],
        keys,
        values,
    )


class Ring:
    def __init__(self, axis):
        self.axis = axis
        if axis == "narrow":
            self.split = lambda i: (i // 2, i % 2, 0)
        else:
            self.split = lambda i: (i // 2 % 4, i // 8, i % 2)
        self.places = [self.split(i) for i in range(lax.axis_size(axis))]
        index_of = {place: i for i, place in enumerate(self.places)}

        def pairs(steps, flip, core):
            return [
                (i, index_of[((r + steps) % 4, p ^ flip, c ^ core)])
                for i, (r, p, c) in enumerate(self.places)
            ]

        self.pairs = pairs
        self.at_ring, self.at_pair, self.at_core = self.split(lax.axis_index(axis))

    def up(self, block):
        return lax.ppermute(block, self.axis, self.pairs(1, 0, 0))

    def down(self, block):
        return lax.ppermute(block, self.axis, self.pairs(-1, 0, 0))

    def swap(self, block):
        return lax.ppermute(block, self.axis, self.pairs(0, 1, 0))

    def cores(self, block):
        return lax.ppermute(block, self.axis, self.pairs(0, 0, 1))

    def ring(self, steps):
        return (self.at_ring + steps) % 4


def place(buffer, block, *index):
    start = tuple(index) + (0,) * (buffer.ndim - len(index))
    shape = (1,) * (buffer.ndim - block.ndim) + block.shape
    return lax.dynamic_update_slice(buffer, block.reshape(shape), start)


def halves(block):
    return block.reshape((2, -1) + block.shape[1:])


def gathered_wide(wide, own_core, other_core):
    block = own_core[0]
    rows, half = block.shape[0], block.shape[0] // 2
    every = jnp.zeros((2, 4, 2, 2, half) + block.shape[1:], block.dtype)
    one, other = wide.at_pair, 1 - wide.at_pair
    for core, pieces in ((wide.at_core, own_core), (1 - wide.at_core, other_core)):
        own, up, down, swap, two_up, two_down, far_up, far_down = pieces
        every = place(every, halves(own), one, wide.ring(0), core)
        every = place(every, halves(up), one, wide.ring(3), core)
        every = place(every, halves(down), one, wide.ring(1), core)
        every = place(every, halves(swap), other, wide.ring(0), core)
        every = place(every, halves(two_up[:rows]), other, wide.ring(3), core)
        every = place(every, halves(two_down[:rows]), other, wide.ring(1), core)
        every = place(every, two_up[rows:], one, wide.ring(2), core, 0)
        every = place(every, two_down[rows:], one, wide.ring(2), core, 1)
        every = place(every, far_up, other, wide.ring(2), core, 0)
        every = place(every, far_down, other, wide.ring(2), core, 1)
    return every.reshape((-1,) + block.shape[1:])


def put_kernel(sources, aliased, places, *refs):
    pieces, result = refs[aliased:-1], refs[-1]
    rows = result.shape[1]
    step = pl.program_id(0)
    for i, (piece, block) in enumerate(sources):

        @pl.when(step == i)
        def _():
            result[0] = pieces[piece][block * rows : (block + 1) * rows]


def put(buffer, pieces, sources, places, blocks, rows, vmem_limit=24 << 20):
    columns = pieces[0].shape[1]
    aliased = 0 if buffer is None else 1
    held = () if buffer is None else (buffer,)
    return pl.pallas_call(
        functools.partial(put_kernel, sources, aliased),
        grid_spec=pltpu.PrefetchScalarGridSpec(
            num_scalar_prefetch=1,
            grid=(len(sources),),
            in_specs=[pl.BlockSpec(memory_space=pl.ANY)] * aliased
            + [pl.BlockSpec(piece.shape, lambda i, *_: (0, 0)) for piece in pieces],
            out_specs=pl.BlockSpec((1, rows, columns), lambda i, places: (places[i], 0, 0)),
        ),
        out_shape=jax.ShapeDtypeStruct((blocks, rows, columns), pieces[0].dtype),
        input_output_aliases={1: 0} if aliased else {},
        compiler_params=pltpu.CompilerParams(vmem_limit_bytes=vmem_limit),
        cost_estimate=pl.CostEstimate(
            flops=0, bytes_accessed=4 * len(sources) * rows * columns, transcendentals=0
        ),
        name="put",
    )(places, *held, *pieces)


def pack_kernel(payloads, pieces, *refs):
    for payload, out in zip(payloads, refs[pieces:]):
        start = 0
        for piece, source, count in payload:
            out[start : start + count] = refs[piece][source : source + count]
            start += count


def pack(pieces, payloads, steps, vmem_limit=8 << 20):
    columns = pieces[0].shape[1]
    rows = [sum(count for _, _, count in payload) for payload in payloads]
    block = lambda count: pl.BlockSpec((count, columns // steps), lambda i: (0, i))
    return pl.pallas_call(
        functools.partial(pack_kernel, tuple(payloads), len(pieces)),
        grid=(steps,),
        in_specs=[block(piece.shape[0]) for piece in pieces],
        out_specs=[block(count) for count in rows],
        out_shape=[jax.ShapeDtypeStruct((count, columns), pieces[0].dtype) for count in rows],
        compiler_params=pltpu.CompilerParams(vmem_limit_bytes=vmem_limit),
        cost_estimate=pl.CostEstimate(
            flops=0, bytes_accessed=4 * sum(rows) * columns, transcendentals=0
        ),
        name="pack",
    )(*pieces)


def shards(
    tokens,
    ln_gain,
    w_qkv,
    q_gain,
    k_gain,
    stored_keys,
    stored_values,
    span_lengths,
    fill_positions,
    w_out,
):
    barrier = lax.optimization_barrier
    wide, narrow = Ring("wide"), Ring("narrow")
    wide_count = lax.axis_size("wide")
    streams = span_lengths.shape[0]
    rows = tokens.shape[0] // lax.axis_size("narrow")
    slots = rows // streams
    depth = w_qkv.shape[0]
    half_rows, half_depth = rows // 2, depth // 2

    own_rows = lax.all_to_all(tokens, "narrow", split_axis=0, concat_axis=1, tiled=True)
    w_up, w_down, w_swap = narrow.up(w_qkv), narrow.down(w_qkv), narrow.swap(w_qkv)
    o_up, o_down = wide.up(w_out), wide.down(w_out)
    token_values = own_rows.astype(jnp.float32)
    own_squares = jnp.sum(token_values * token_values, axis=1)
    normed = (token_values * ln_gain[None, :]).astype(jnp.bfloat16)
    w_up, w_down, w_swap, o_up, o_down, normed = barrier(
        (w_up, w_down, w_swap, o_up, o_down, normed)
    )

    w_swap_up, w_swap_down = narrow.up(w_swap), narrow.down(w_swap)
    t_up, t_down, t_swap = wide.up(normed), wide.down(normed), wide.swap(normed)
    inverse = jnp.broadcast_to(lax.rsqrt(own_squares / D + EPSILON)[:, None], (rows, HEAD_SIZE))
    cosine, sine = turn_tables(fill_positions, slots)
    w_swap_up, w_swap_down, t_up, t_down, t_swap, inverse, cosine, sine = barrier(
        (w_swap_up, w_swap_down, t_up, t_down, t_swap, inverse, cosine, sine)
    )

    w_far_up = narrow.up(jnp.concatenate([w_up[:half_depth], w_swap_up[:half_depth]]))
    w_far_down = narrow.down(jnp.concatenate([w_down[half_depth:], w_swap_down[half_depth:]]))
    t_two_up = wide.up(jnp.concatenate([t_swap, t_up[:half_rows]]))
    t_two_down = wide.down(jnp.concatenate([t_swap, t_down[half_rows:]]))
    near = wide.cores(jnp.stack([normed, t_up, t_down, t_swap]))
    t_two_up, t_two_down, w_far_up, w_far_down, near = barrier(
        (t_two_up, t_two_down, w_far_up, w_far_down, near)
    )

    t_far_up = wide.up(t_two_up[:half_rows])
    t_far_down = wide.down(t_two_down[half_rows:rows])
    o_swap = wide.swap(w_out)
    two = wide.cores(jnp.stack([t_two_up, t_two_down]))
    far = wide.cores(jnp.stack([t_far_up, t_far_down]))

    columns = jnp.zeros((4, 2, 2, half_depth) + w_qkv.shape[1:], w_qkv.dtype)
    one, other = narrow.at_pair, 1 - narrow.at_pair
    columns = place(columns, halves(w_qkv), narrow.ring(0), one)
    columns = place(columns, halves(w_up), narrow.ring(3), one)
    columns = place(columns, halves(w_down), narrow.ring(1), one)
    columns = place(columns, halves(w_swap), narrow.ring(0), other)
    columns = place(columns, halves(w_swap_up), narrow.ring(3), other)
    columns = place(columns, halves(w_swap_down), narrow.ring(1), other)
    w_far_up, w_far_down = halves(w_far_up), halves(w_far_down)
    columns = place(columns, w_far_up[0], narrow.ring(2), one, 0)
    columns = place(columns, w_far_down[0], narrow.ring(2), one, 1)
    columns = place(columns, w_far_up[1], narrow.ring(2), other, 0)
    columns = place(columns, w_far_down[1], narrow.ring(2), other, 1)
    columns = columns.reshape(-1, w_qkv.shape[1])

    every = gathered_wide(
        wide,
        (normed, t_up, t_down, t_swap, t_two_up, t_two_down, t_far_up, t_far_down),
        (*near, *two, *far),
    )

    every, columns, o_swap = barrier((every, columns, o_swap))
    projected = jnp.dot(every, columns, preferred_element_type=jnp.float32).astype(jnp.bfloat16)
    packed = lax.all_to_all(
        projected.reshape(wide_count, rows, -1), "wide", split_axis=0, concat_axis=0, tiled=True
    )
    packed, o_swap, o_up, o_down = barrier((packed, o_swap, o_up, o_down))

    out_rows = w_out.shape[0]
    half_out = out_rows // 2
    o_two_up = wide.up(jnp.concatenate([o_swap, o_up[:half_out]]))
    o_two_down = wide.down(jnp.concatenate([o_swap, o_down[half_out:]]))
    attended = attend(
        packed,
        inverse,
        cosine,
        sine,
        q_gain,
        k_gain,
        stored_keys,
        stored_values,
        span_lengths,
        fill_positions,
    )

    quarter = rows // 4
    attended, w_out, o_up, o_down, o_swap = barrier((attended, w_out, o_up, o_down, o_swap))
    a_up, a_down, a_swap = narrow.up(attended), narrow.down(attended), narrow.swap(attended)
    o_far_up = wide.up(o_two_up[:half_out])
    o_far_down = wide.down(o_two_down[half_out:out_rows])
    o_near, o_rest = pack(
        (w_out, o_up, o_down, o_swap, o_two_up, o_two_down, o_far_up, o_far_down),
        (
            tuple((i, 0, out_rows) for i in range(4)),
            ((4, 0, 3 * half_out), (5, 0, 3 * half_out), (6, 0, half_out), (7, 0, half_out)),
        ),
        5,
        12 << 20,
    )
    a_up, a_down, a_swap, o_far_up, o_far_down, o_near, o_rest = barrier(
        (a_up, a_down, a_swap, o_far_up, o_far_down, o_near, o_rest)
    )

    b_up, b_down, b_swap = pack(
        (a_up, a_down, a_swap),
        (
            ((2, half_rows, half_rows), (0, 0, half_rows)),
            ((2, half_rows, half_rows), (1, half_rows, half_rows)),
            ((0, 0, half_rows), (1, 0, half_rows)),
        ),
        4,
    )
    b_up, b_down, b_swap = narrow.up(b_up), narrow.down(b_down), narrow.swap(b_swap)
    o_near = wide.cores(o_near)
    o_rest = wide.cores(o_rest)
    chips = tuple(
        (pair * 4 + wide.ring(ring)) * 2
        for ring, pair in (
            (0, wide.at_pair),
            (3, wide.at_pair),
            (1, wide.at_pair),
            (0, 1 - wide.at_pair),
            (3, 1 - wide.at_pair),
            (1, 1 - wide.at_pair),
            (2, wide.at_pair),
            (2, 1 - wide.at_pair),
        )
    )
    every_w_out = put(
        None,
        (w_out, o_up, o_down, o_swap, o_two_up, o_two_down, o_far_up, o_far_down),
        tuple((i, half) for i in range(6) for half in range(2))
        + ((4, 2), (5, 2), (6, 0), (7, 0)),
        jnp.stack([(chip + wide.at_core) * 2 + half for chip in chips for half in range(2)]),
        wide_count * 2,
        half_out,
    )
    every_w_out = put(
        every_w_out,
        (o_near, o_rest),
        tuple((0, i) for i in range(8)) + tuple((1, i) for i in (0, 1, 3, 4, 2, 5, 6, 7)),
        jnp.stack([(chip + 1 - wide.at_core) * 2 + half for chip in chips for half in range(2)]),
        wide_count * 2,
        half_out,
    ).reshape(-1, w_out.shape[1])

    def project_out(part):
        product = jnp.dot(part, every_w_out, preferred_element_type=jnp.float32)
        return product.astype(jnp.bfloat16)

    near_rows = project_out(jnp.concatenate([attended, a_swap, a_up, a_down]))
    b_up, b_down, b_swap, near_rows = barrier((b_up, b_down, b_swap, near_rows))
    c_up = narrow.up(b_up[:quarter])
    c_down = narrow.down(b_down[quarter:half_rows])
    c_swap = narrow.swap(b_up[half_rows:])
    one, other = narrow.at_pair, 1 - narrow.at_pair
    place_of = lambda ring, pair, half: (narrow.ring(ring) * 2 + pair) * 2 + half
    result = put(
        None,
        (near_rows, project_out(jnp.concatenate([b_swap, b_up, b_down]))),
        tuple((0, i) for i in range(8)) + tuple((1, i) for i in range(6)),
        jnp.stack(
            [
                place_of(ring, pair, half)
                for ring, pair in ((0, one), (0, other), (3, one), (1, one))
                for half in range(2)
            ]
            + [
                place_of(*place)
                for place in (
                    (3, other, 0),
                    (1, other, 0),
                    (3, other, 1),
                    (2, one, 0),
                    (1, other, 1),
                    (2, one, 1),
                )
            ]
        ),
        16,
        half_rows,
    )
    result, c_up, c_down, c_swap = barrier((result, c_up, c_down, c_swap))
    result = put(
        result,
        (project_out(jnp.concatenate([c_swap, c_up, c_down])),),
        ((0, 0), (0, 1)),
        jnp.stack([place_of(2, other, 0), place_of(2, other, 1)]),
        16,
        half_rows,
    )
    return result.reshape(-1, result.shape[-1])


def solution(mesh):
    placed = (
        P("wide", "narrow"),
        P(),
        P("narrow", "wide"),
        P(),
        P(),
        P(("wide", "narrow"), None, None),
        P(("wide", "narrow"), None, None),
        P(("wide", "narrow")),
        P(("wide", "narrow")),
        P("wide", "narrow"),
    )
    return jax.shard_map(
        shards, mesh=mesh, in_specs=placed, out_specs=P("wide", "narrow"), check_vma=False
    )
```

```python
import functools
import math

import jax
import jax.numpy as jnp
from jax import lax
from jax.experimental import pallas as pl
from jax.experimental.pallas import tpu as pltpu
from jax.sharding import PartitionSpec as P

D = 5120
QUERY_HEADS = 64
KEY_VALUE_HEADS = 8
HEAD_SIZE = 128


EPSILON = 1e-06
ROPE_BASE = 1000000.0


def turn_tables(fill_positions, slots):
    half = HEAD_SIZE // 2
    slot_index = jnp.arange(slots, dtype=jnp.int32)
    position = (fill_positions[:, None] + slot_index[None, :]).reshape(-1).astype(jnp.float32)
    frequency = jnp.exp(
        jnp.arange(half, dtype=jnp.float32) * (-2.0 * math.log(ROPE_BASE) / HEAD_SIZE)
    )
    angles = position[:, None] * frequency[None, :]
    cosine, sine = jnp.cos(angles), jnp.sin(angles)
    return (
        jnp.concatenate([cosine, cosine], axis=1),
        jnp.concatenate([-sine, sine], axis=1),
    )


def attend_kernel(
    fills,
    spans,
    packed,
    inverse,
    cosine,
    sine,
    q_gain,
    k_gain,
    keys,
    values,
    attended,
):
    stream = pl.program_id(0)
    fill, span = fills[stream], spans[stream]
    slots = packed.shape[1]
    frames = keys.shape[1]
    group = QUERY_HEADS // KEY_VALUE_HEADS
    rows = group * slots
    cos_one, sin_one = cosine[...], sine[...]

    def turned(vectors, gains, cos_rows, sin_rows):
        mean_square = jnp.mean(vectors * vectors, axis=-1, keepdims=True)
        normed = vectors * lax.rsqrt(mean_square + EPSILON) * gains
        swapped = pltpu.roll(normed, HEAD_SIZE // 2, 1)
        return (normed * cos_rows + swapped * sin_rows).astype(jnp.bfloat16)

    cos_all = jnp.concatenate([cos_one] * group, axis=0)
    sin_all = jnp.concatenate([sin_one] * group, axis=0)
    low = lax.broadcasted_iota(jnp.int32, (slots, HEAD_SIZE), 1) < HEAD_SIZE // 2
    frame_live = lax.broadcasted_iota(jnp.int32, (rows, frames), 1) < fill
    slot_row = lax.broadcasted_iota(jnp.int32, (group, slots, HEAD_SIZE), 1)
    slot_row = slot_row.reshape(rows, HEAD_SIZE)
    slot_column = lax.broadcasted_iota(jnp.int32, (rows, HEAD_SIZE), 1)
    slot_live = (slot_column <= slot_row) & (slot_column < span)
    row_live = slot_row < span
    empty = jnp.zeros((HEAD_SIZE - slots, HEAD_SIZE), jnp.bfloat16)
    query_columns = group // 2 * HEAD_SIZE
    contract_last = (((1,), (1,)), ((), ()))
    score_scale = 1.0 / math.sqrt(HEAD_SIZE)
    for head in range(KEY_VALUE_HEADS):
        queries = jnp.concatenate(
            [
                packed[2 * head + g // 4, :, g % 4 * HEAD_SIZE : (g % 4 + 1) * HEAD_SIZE]
                for g in range(group)
            ],
            axis=0,
        ).astype(jnp.float32)
        queries = turned(queries, q_gain[...], cos_all, sin_all)
        first = packed[2 * head, :, query_columns:].astype(jnp.float32)
        second = packed[2 * head + 1, :, query_columns:].astype(jnp.float32)
        fresh_key = jnp.where(low, first, pltpu.roll(second, HEAD_SIZE // 2, 1))
        fresh_value = jnp.where(low, pltpu.roll(first, HEAD_SIZE // 2, 1), second)
        fresh_key = jnp.concatenate([turned(fresh_key, k_gain[...], cos_one, sin_one), empty])
        fresh_value = jnp.concatenate([(fresh_value * inverse[...]).astype(jnp.bfloat16), empty])
        columns = slice(head * HEAD_SIZE, (head + 1) * HEAD_SIZE)
        old = lax.dot_general(
            queries, keys[0, :, columns], contract_last, preferred_element_type=jnp.float32
        )
        new = lax.dot_general(
            queries, fresh_key, contract_last, preferred_element_type=jnp.float32
        )
        old = jnp.where(frame_live, old * score_scale, -1e30)
        new = jnp.where(slot_live, new * score_scale, -1e30)
        scores = jnp.concatenate([old, new], axis=1)
        weights = jnp.exp(scores - jnp.max(scores, axis=-1, keepdims=True))
        total = jnp.sum(weights, axis=-1, keepdims=True)
        weights = weights.astype(jnp.bfloat16)
        mixed = jnp.dot(
            weights[:, :frames], values[0, :, columns], preferred_element_type=jnp.float32
        ) + jnp.dot(weights[:, frames:], fresh_value, preferred_element_type=jnp.float32)
        mixed = jnp.where(row_live, mixed / total, 0.0).astype(jnp.bfloat16)
        for g in range(group):
            start = (head * group + g) * HEAD_SIZE
            attended[:, start : start + HEAD_SIZE] = mixed[g * slots : (g + 1) * slots]


def attend(packed, inverse, cosine, sine, q_gain, k_gain, keys, values, spans, fills):
    groups, rows, columns = packed.shape
    streams, frames, width = keys.shape
    slots = rows // streams
    heads = QUERY_HEADS * HEAD_SIZE
    tables = pl.BlockSpec((slots, HEAD_SIZE), lambda s, *_: (s, 0))
    gains = pl.BlockSpec((1, HEAD_SIZE), lambda s, *_: (0, 0))
    cache = pl.BlockSpec((1, frames, width), lambda s, *_: (s, 0, 0))
    return pl.pallas_call(
        attend_kernel,
        grid_spec=pltpu.PrefetchScalarGridSpec(
            num_scalar_prefetch=2,
            grid=(streams,),
            in_specs=[
                pl.BlockSpec((groups, slots, columns), lambda s, *_: (0, s, 0)),
                tables,
                tables,
                tables,
                gains,
                gains,
                cache,
                cache,
            ],
            out_specs=pl.BlockSpec((slots, heads), lambda s, *_: (s, 0)),
        ),
        out_shape=jax.ShapeDtypeStruct((rows, heads), jnp.bfloat16),
        compiler_params=pltpu.CompilerParams(vmem_limit_bytes=24 << 20),
        cost_estimate=pl.CostEstimate(
            flops=4 * rows * heads * (frames + slots),
            bytes_accessed=4 * streams * frames * width + 4 * rows * 9216,
            transcendentals=rows * QUERY_HEADS * (frames + slots),
        ),
        name="attend",
    )(
        fills,
        spans,
        packed,
        inverse,
        cosine,
        sine,
        q_gain[None],
        k_gain[None],
        keys,
        values,
    )


class Ring:
    def __init__(self, axis):
        self.axis = axis
        if axis == "narrow":
            self.split = lambda i: (i // 2, i % 2, 0)
        else:
            self.split = lambda i: (i // 2 % 4, i // 8, i % 2)
        self.places = [self.split(i) for i in range(lax.axis_size(axis))]
        index_of = {place: i for i, place in enumerate(self.places)}

        def pairs(steps, flip, core):
            return [
                (i, index_of[((r + steps) % 4, p ^ flip, c ^ core)])
                for i, (r, p, c) in enumerate(self.places)
            ]

        self.pairs = pairs
        self.at_ring, self.at_pair, self.at_core = self.split(lax.axis_index(axis))

    def up(self, block):
        return lax.ppermute(block, self.axis, self.pairs(1, 0, 0))

    def down(self, block):
        return lax.ppermute(block, self.axis, self.pairs(-1, 0, 0))

    def swap(self, block):
        return lax.ppermute(block, self.axis, self.pairs(0, 1, 0))

    def cores(self, block):
        return lax.ppermute(block, self.axis, self.pairs(0, 0, 1))

    def ring(self, steps):
        return (self.at_ring + steps) % 4


def place(buffer, block, *index):
    start = tuple(index) + (0,) * (buffer.ndim - len(index))
    shape = (1,) * (buffer.ndim - block.ndim) + block.shape
    return lax.dynamic_update_slice(buffer, block.reshape(shape), start)


def halves(block):
    return block.reshape((2, -1) + block.shape[1:])


def put_kernel(sources, aliased, places, *refs):
    pieces, result = refs[aliased:-1], refs[-1]
    rows = result.shape[1]
    step = pl.program_id(0)
    for i, (piece, block) in enumerate(sources):

        @pl.when(step == i)
        def _():
            result[0] = pieces[piece][block * rows : (block + 1) * rows]


def put(buffer, pieces, sources, places, blocks, rows, vmem_limit=24 << 20):
    columns = pieces[0].shape[1]
    aliased = 0 if buffer is None else 1
    held = () if buffer is None else (buffer,)
    return pl.pallas_call(
        functools.partial(put_kernel, sources, aliased),
        grid_spec=pltpu.PrefetchScalarGridSpec(
            num_scalar_prefetch=1,
            grid=(len(sources),),
            in_specs=[pl.BlockSpec(memory_space=pl.ANY)] * aliased
            + [pl.BlockSpec(piece.shape, lambda i, *_: (0, 0)) for piece in pieces],
            out_specs=pl.BlockSpec((1, rows, columns), lambda i, places: (places[i], 0, 0)),
        ),
        out_shape=jax.ShapeDtypeStruct((blocks, rows, columns), pieces[0].dtype),
        input_output_aliases={1: 0} if aliased else {},
        compiler_params=pltpu.CompilerParams(vmem_limit_bytes=vmem_limit),
        cost_estimate=pl.CostEstimate(flops=0, bytes_accessed=rows, transcendentals=0),
        name="put",
    )(places, *held, *pieces)


def pack_kernel(payloads, pieces, *refs):
    for payload, out in zip(payloads, refs[pieces:]):
        start = 0
        for piece, source, count in payload:
            out[start : start + count] = refs[piece][source : source + count]
            start += count


def pack(pieces, payloads, steps, vmem_limit=8 << 20):
    columns = pieces[0].shape[1]
    rows = [sum(count for _, _, count in payload) for payload in payloads]
    block = lambda count: pl.BlockSpec((count, columns // steps), lambda i: (0, i))
    return pl.pallas_call(
        functools.partial(pack_kernel, tuple(payloads), len(pieces)),
        grid=(steps,),
        in_specs=[block(piece.shape[0]) for piece in pieces],
        out_specs=[block(count) for count in rows],
        out_shape=[jax.ShapeDtypeStruct((count, columns), pieces[0].dtype) for count in rows],
        compiler_params=pltpu.CompilerParams(vmem_limit_bytes=vmem_limit),
        cost_estimate=pl.CostEstimate(flops=0, bytes_accessed=sum(rows), transcendentals=0),
        name="pack",
    )(*pieces)


def shards(
    tokens,
    ln_gain,
    w_qkv,
    q_gain,
    k_gain,
    stored_keys,
    stored_values,
    span_lengths,
    fill_positions,
    w_out,
):
    barrier = lax.optimization_barrier
    wide, narrow = Ring("wide"), Ring("narrow")
    wide_count = lax.axis_size("wide")
    streams = span_lengths.shape[0]
    rows = tokens.shape[0] // lax.axis_size("narrow")
    slots = rows // streams
    depth = w_qkv.shape[0]
    half_rows, half_depth = rows // 2, depth // 2

    own_rows = lax.all_to_all(tokens, "narrow", split_axis=0, concat_axis=1, tiled=True)
    w_up, w_down, w_swap = narrow.up(w_qkv), narrow.down(w_qkv), narrow.swap(w_qkv)
    o_up, o_down = wide.up(w_out), wide.down(w_out)
    token_values = own_rows.astype(jnp.float32)
    own_squares = jnp.sum(token_values * token_values, axis=1)
    normed = (token_values * ln_gain[None, :]).astype(jnp.bfloat16)
    o_up, o_down, w_swap, w_up, w_down, normed = barrier(
        (o_up, o_down, w_swap, w_up, w_down, normed)
    )

    w_swap_up, w_swap_down = narrow.up(w_swap), narrow.down(w_swap)
    t_up, t_down, t_swap = wide.up(normed), wide.down(normed), wide.swap(normed)
    inverse = jnp.broadcast_to(lax.rsqrt(own_squares / D + EPSILON)[:, None], (rows, HEAD_SIZE))
    cosine, sine = turn_tables(fill_positions, slots)
    one, other = wide.at_pair, 1 - wide.at_pair
    every = jnp.zeros((2, 4, 2, 2, half_rows) + normed.shape[1:], normed.dtype)
    every = place(every, halves(normed), one, wide.ring(0), wide.at_core)
    w_swap_up, w_swap_down, t_up, t_down, t_swap, inverse, cosine, sine, every = barrier(
        (w_swap_up, w_swap_down, t_up, t_down, t_swap, inverse, cosine, sine, every)
    )

    w_far_up = narrow.up(jnp.concatenate([w_up[:half_depth], w_swap_up[:half_depth]]))
    w_far_down = narrow.down(jnp.concatenate([w_down[half_depth:], w_swap_down[half_depth:]]))
    t_two_up = wide.up(jnp.concatenate([t_swap, t_up[:half_rows]]))
    t_two_down = wide.down(jnp.concatenate([t_swap, t_down[half_rows:]]))
    o_swap = wide.swap(w_out)
    near = jnp.stack([normed, t_up, t_down, t_swap])
    at_narrow = tuple(
        narrow.ring(ring) * 2 + pair
        for pair in (narrow.at_pair, 1 - narrow.at_pair)
        for ring in (0, 3, 1, 2)
    )
    columns = put(
        None,
        (w_qkv, w_up, w_down, w_swap, w_swap_up, w_swap_down),
        tuple((i, half) for i in range(6) for half in range(2)),
        jnp.stack([at_narrow[i] * 2 + half for i in (0, 1, 2, 4, 5, 6) for half in range(2)]),
        16,
        half_depth,
    )
    every = place(every, halves(t_up), one, wide.ring(3), wide.at_core)
    every = place(every, halves(t_down), one, wide.ring(1), wide.at_core)
    every = place(every, halves(t_swap), other, wide.ring(0), wide.at_core)
    w_far_up, w_far_down, t_two_up, t_two_down, o_swap, near, columns, every = barrier(
        (w_far_up, w_far_down, t_two_up, t_two_down, o_swap, near, columns, every)
    )

    t_far_up = wide.up(t_two_up[:half_rows])
    t_far_down = wide.down(t_two_down[half_rows:rows])
    near = wide.cores(near)
    two = wide.cores(jnp.stack([t_two_up, t_two_down]))
    far = wide.cores(jnp.stack([t_far_up, t_far_down]))
    columns = put(
        columns,
        (w_far_up, w_far_down),
        ((0, 0), (1, 0), (0, 1), (1, 1)),
        jnp.stack([at_narrow[i] * 2 + half for i in (3, 7) for half in range(2)]),
        16,
        half_depth,
    ).reshape(-1, w_qkv.shape[1])
    for core, (two_up, two_down), (far_up, far_down) in (
        (wide.at_core, (t_two_up, t_two_down), (t_far_up, t_far_down)),
        (1 - wide.at_core, two, far),
    ):
        every = place(every, halves(two_up[:rows]), other, wide.ring(3), core)
        every = place(every, halves(two_down[:rows]), other, wide.ring(1), core)
        every = place(every, two_up[rows:], one, wide.ring(2), core, 0)
        every = place(every, two_down[rows:], one, wide.ring(2), core, 1)
        every = place(every, far_up, other, wide.ring(2), core, 0)
        every = place(every, far_down, other, wide.ring(2), core, 1)
    for block, pair, ring in zip(near, (one, one, one, other), (0, 3, 1, 0)):
        every = place(every, halves(block), pair, wide.ring(ring), 1 - wide.at_core)
    every = every.reshape(-1, normed.shape[1])
    every, columns = barrier((every, columns))
    projected = jnp.dot(every, columns, preferred_element_type=jnp.float32).astype(jnp.bfloat16)
    packed = lax.all_to_all(
        projected.reshape(wide_count, rows, -1), "wide", split_axis=0, concat_axis=0, tiled=True
    )
    packed, o_swap, o_up, o_down = barrier((packed, o_swap, o_up, o_down))

    out_rows = w_out.shape[0]
    half_out = out_rows // 2
    o_two_up = wide.up(jnp.concatenate([o_swap, o_up[:half_out]]))
    o_two_down = wide.down(jnp.concatenate([o_swap, o_down[half_out:]]))
    attended = attend(
        packed,
        inverse,
        cosine,
        sine,
        q_gain,
        k_gain,
        stored_keys,
        stored_values,
        span_lengths,
        fill_positions,
    )

    quarter = rows // 4
    attended, w_out, o_up, o_down, o_swap = barrier((attended, w_out, o_up, o_down, o_swap))
    a_up, a_down, a_swap = narrow.up(attended), narrow.down(attended), narrow.swap(attended)
    o_far_up = wide.up(o_two_up[:half_out])
    o_far_down = wide.down(o_two_down[half_out:out_rows])
    (o_near,) = pack(
        (w_out, o_up, o_down, o_swap, o_two_up, o_two_down),
        (
            tuple((i, 0, out_rows) for i in range(4))
            + tuple((i, 0, 3 * half_out) for i in (4, 5)),
        ),
        5,
        12 << 20,
    )
    other_far = jnp.stack([o_far_up, o_far_down])
    a_up, a_down, a_swap, o_far_up, o_far_down, o_near, other_far = barrier(
        (a_up, a_down, a_swap, o_far_up, o_far_down, o_near, other_far)
    )

    b_up = narrow.up(jnp.concatenate([a_swap[half_rows:], a_up[:half_rows]]))
    b_down = narrow.down(jnp.concatenate([a_swap[half_rows:], a_down[half_rows:]]))
    b_swap = narrow.swap(jnp.concatenate([a_up[:half_rows], a_down[:half_rows]]))
    o_near = wide.cores(o_near)
    other_far = wide.cores(other_far).reshape(out_rows, -1)
    chips = tuple(
        (pair * 4 + wide.ring(ring)) * 2
        for ring, pair in (
            (0, wide.at_pair),
            (3, wide.at_pair),
            (1, wide.at_pair),
            (0, 1 - wide.at_pair),
            (3, 1 - wide.at_pair),
            (1, 1 - wide.at_pair),
            (2, wide.at_pair),
            (2, 1 - wide.at_pair),
        )
    )
    every_w_out = put(
        None,
        (w_out, o_up, o_down, o_swap, o_two_up, o_two_down, o_far_up, o_far_down),
        tuple((i, half) for i in range(6) for half in range(2))
        + ((4, 2), (5, 2), (6, 0), (7, 0)),
        jnp.stack([(chip + wide.at_core) * 2 + half for chip in chips for half in range(2)]),
        wide_count * 2,
        half_out,
    )
    every_w_out = put(
        every_w_out,
        (o_near, other_far),
        tuple((0, i) for i in (0, 1, 2, 3, 4, 5, 6, 7, 8, 9, 11, 12, 10, 13)) + ((1, 0), (1, 1)),
        jnp.stack([(chip + 1 - wide.at_core) * 2 + half for chip in chips for half in range(2)]),
        wide_count * 2,
        half_out,
    ).reshape(-1, w_out.shape[1])

    def project_out(part):
        product = jnp.dot(part, every_w_out, preferred_element_type=jnp.float32)
        return product.astype(jnp.bfloat16)

    near_rows = project_out(jnp.concatenate([attended, a_swap, a_up, a_down]))
    b_up, b_down, b_swap, near_rows = barrier((b_up, b_down, b_swap, near_rows))
    c_up = narrow.up(b_up[:quarter])
    c_down = narrow.down(b_down[quarter:half_rows])
    c_swap = narrow.swap(b_up[half_rows:])
    one, other = narrow.at_pair, 1 - narrow.at_pair
    place_of = lambda ring, pair, half: (narrow.ring(ring) * 2 + pair) * 2 + half
    result = put(
        None,
        (near_rows, project_out(jnp.concatenate([b_swap, b_up, b_down]))),
        tuple((0, i) for i in range(8)) + tuple((1, i) for i in range(6)),
        jnp.stack(
            [
                place_of(ring, pair, half)
                for ring, pair in ((0, one), (0, other), (3, one), (1, one))
                for half in range(2)
            ]
            + [
                place_of(*place)
                for place in (
                    (3, other, 0),
                    (1, other, 0),
                    (3, other, 1),
                    (2, one, 0),
                    (1, other, 1),
                    (2, one, 1),
                )
            ]
        ),
        16,
        half_rows,
    )
    result, c_up, c_down, c_swap = barrier((result, c_up, c_down, c_swap))
    result = put(
        result,
        (project_out(jnp.concatenate([c_swap, c_up, c_down])),),
        ((0, 0), (0, 1)),
        jnp.stack([place_of(2, other, 0), place_of(2, other, 1)]),
        16,
        half_rows,
    )
    return result.reshape(-1, result.shape[-1])


def solution(mesh):
    placed = (
        P("wide", "narrow"),
        P(),
        P("narrow", "wide"),
        P(),
        P(),
        P(("wide", "narrow"), None, None),
        P(("wide", "narrow"), None, None),
        P(("wide", "narrow")),
        P(("wide", "narrow")),
        P("wide", "narrow"),
    )
    return jax.shard_map(
        shards, mesh=mesh, in_specs=placed, out_specs=P("wide", "narrow"), check_vma=False
    )
```

```python
import functools
import math

import jax
import jax.numpy as jnp
from jax import lax
from jax.experimental import pallas as pl
from jax.experimental.pallas import tpu as pltpu
from jax.sharding import PartitionSpec as P

D = 5120
QUERY_HEADS = 64
KEY_VALUE_HEADS = 8
HEAD_SIZE = 128


EPSILON = 1e-06
ROPE_BASE = 1000000.0


def turn_tables(fill_positions, slots):
    half = HEAD_SIZE // 2
    slot_index = jnp.arange(slots, dtype=jnp.int32)
    position = (fill_positions[:, None] + slot_index[None, :]).reshape(-1).astype(jnp.float32)
    frequency = jnp.exp(
        jnp.arange(half, dtype=jnp.float32) * (-2.0 * math.log(ROPE_BASE) / HEAD_SIZE)
    )
    angles = position[:, None] * frequency[None, :]
    cosine, sine = jnp.cos(angles), jnp.sin(angles)
    return (
        jnp.concatenate([cosine, cosine], axis=1),
        jnp.concatenate([-sine, sine], axis=1),
    )


def attend_kernel(
    fills,
    spans,
    packed,
    inverse,
    cosine,
    sine,
    q_gain,
    k_gain,
    keys,
    values,
    attended,
):
    stream = pl.program_id(0)
    fill, span = fills[stream], spans[stream]
    slots = packed.shape[1]
    frames = keys.shape[1]
    group = QUERY_HEADS // KEY_VALUE_HEADS
    rows = group * slots
    cos_one, sin_one = cosine[...], sine[...]

    def turned(vectors, gains, cos_rows, sin_rows):
        mean_square = jnp.mean(vectors * vectors, axis=-1, keepdims=True)
        normed = vectors * lax.rsqrt(mean_square + EPSILON) * gains
        swapped = pltpu.roll(normed, HEAD_SIZE // 2, 1)
        return (normed * cos_rows + swapped * sin_rows).astype(jnp.bfloat16)

    cos_all = jnp.concatenate([cos_one] * group, axis=0)
    sin_all = jnp.concatenate([sin_one] * group, axis=0)
    low = lax.broadcasted_iota(jnp.int32, (slots, HEAD_SIZE), 1) < HEAD_SIZE // 2
    frame_live = lax.broadcasted_iota(jnp.int32, (rows, frames), 1) < fill
    slot_row = lax.broadcasted_iota(jnp.int32, (group, slots, HEAD_SIZE), 1)
    slot_row = slot_row.reshape(rows, HEAD_SIZE)
    slot_column = lax.broadcasted_iota(jnp.int32, (rows, HEAD_SIZE), 1)
    slot_live = (slot_column <= slot_row) & (slot_column < span)
    row_live = slot_row < span
    empty = jnp.zeros((HEAD_SIZE - slots, HEAD_SIZE), jnp.bfloat16)
    query_columns = group // 2 * HEAD_SIZE
    contract_last = (((1,), (1,)), ((), ()))
    exp_scale = math.log2(math.e) / math.sqrt(HEAD_SIZE)
    def prepare(head):
        queries = jnp.concatenate(
            [
                packed[2 * head + g // 4, :, g % 4 * HEAD_SIZE : (g % 4 + 1) * HEAD_SIZE]
                for g in range(group)
            ],
            axis=0,
        ).astype(jnp.float32)
        queries = turned(queries, q_gain[...], cos_all, sin_all)
        first = packed[2 * head, :, query_columns:].astype(jnp.float32)
        second = packed[2 * head + 1, :, query_columns:].astype(jnp.float32)
        fresh_key = jnp.where(low, first, pltpu.roll(second, HEAD_SIZE // 2, 1))
        fresh_value = jnp.where(low, pltpu.roll(first, HEAD_SIZE // 2, 1), second)
        fresh_key = jnp.concatenate([turned(fresh_key, k_gain[...], cos_one, sin_one), empty])
        fresh_value = jnp.concatenate([(fresh_value * inverse[...]).astype(jnp.bfloat16), empty])
        return queries, fresh_key, fresh_value

    def score(head, queries, fresh_key):
        columns = slice(head * HEAD_SIZE, (head + 1) * HEAD_SIZE)
        old = lax.dot_general(
            queries, keys[0, :, columns], contract_last, preferred_element_type=jnp.float32
        )
        new = lax.dot_general(
            queries, fresh_key, contract_last, preferred_element_type=jnp.float32
        )
        return old, new

    def weigh(old, new):
        old = jnp.where(frame_live, old, -1e30)
        new = jnp.where(slot_live, new, -1e30)
        scores = jnp.concatenate([old, new], axis=1)
        weights = jnp.exp2((scores - jnp.max(scores, axis=-1, keepdims=True)) * exp_scale)
        return weights.astype(jnp.bfloat16), jnp.sum(weights, axis=-1, keepdims=True)

    def mix(head, weights, total, fresh_value):
        columns = slice(head * HEAD_SIZE, (head + 1) * HEAD_SIZE)
        mixed = jnp.dot(
            weights[:, :frames], values[0, :, columns], preferred_element_type=jnp.float32
        ) + jnp.dot(weights[:, frames:], fresh_value, preferred_element_type=jnp.float32)
        mixed = jnp.where(row_live, mixed / total, 0.0).astype(jnp.bfloat16)
        for g in range(group):
            start = (head * group + g) * HEAD_SIZE
            attended[:, start : start + HEAD_SIZE] = mixed[g * slots : (g + 1) * slots]

    for pair in range(0, KEY_VALUE_HEADS, 2):
        heads = (pair, pair + 1)
        prepared = [prepare(head) for head in heads]
        scored = [score(head, p[0], p[1]) for head, p in zip(heads, prepared)]
        weighed = [weigh(*s) for s in scored]
        for head, w, p in zip(heads, weighed, prepared):
            mix(head, *w, p[2])


def attend(packed, inverse, cosine, sine, q_gain, k_gain, keys, values, spans, fills):
    groups, rows, columns = packed.shape
    streams, frames, width = keys.shape
    slots = rows // streams
    heads = QUERY_HEADS * HEAD_SIZE
    tables = pl.BlockSpec((slots, HEAD_SIZE), lambda s, *_: (s, 0))
    gains = pl.BlockSpec((1, HEAD_SIZE), lambda s, *_: (0, 0))
    cache = pl.BlockSpec((1, frames, width), lambda s, *_: (s, 0, 0))
    return pl.pallas_call(
        attend_kernel,
        grid_spec=pltpu.PrefetchScalarGridSpec(
            num_scalar_prefetch=2,
            grid=(streams,),
            in_specs=[
                pl.BlockSpec((groups, slots, columns), lambda s, *_: (0, s, 0)),
                tables,
                tables,
                tables,
                gains,
                gains,
                cache,
                cache,
            ],
            out_specs=pl.BlockSpec((slots, heads), lambda s, *_: (s, 0)),
        ),
        out_shape=jax.ShapeDtypeStruct((rows, heads), jnp.bfloat16),
        compiler_params=pltpu.CompilerParams(vmem_limit_bytes=24 << 20),
        cost_estimate=pl.CostEstimate(
            flops=4 * rows * heads * (frames + slots),
            bytes_accessed=4 * streams * frames * width + 4 * rows * 9216,
            transcendentals=rows * QUERY_HEADS * (frames + slots),
        ),
        name="attend",
    )(
        fills,
        spans,
        packed,
        inverse,
        cosine,
        sine,
        q_gain[None],
        k_gain[None],
        keys,
        values,
    )


class Ring:
    def __init__(self, axis):
        self.axis = axis
        if axis == "narrow":
            self.split = lambda i: (i // 2, i % 2, 0)
        else:
            self.split = lambda i: (i // 2 % 4, i // 8, i % 2)
        self.places = [self.split(i) for i in range(lax.axis_size(axis))]
        index_of = {place: i for i, place in enumerate(self.places)}

        def pairs(steps, flip, core):
            return [
                (i, index_of[((r + steps) % 4, p ^ flip, c ^ core)])
                for i, (r, p, c) in enumerate(self.places)
            ]

        self.pairs = pairs
        self.at_ring, self.at_pair, self.at_core = self.split(lax.axis_index(axis))

    def up(self, block):
        return lax.ppermute(block, self.axis, self.pairs(1, 0, 0))

    def down(self, block):
        return lax.ppermute(block, self.axis, self.pairs(-1, 0, 0))

    def swap(self, block):
        return lax.ppermute(block, self.axis, self.pairs(0, 1, 0))

    def cores(self, block):
        return lax.ppermute(block, self.axis, self.pairs(0, 0, 1))

    def ring(self, steps):
        return (self.at_ring + steps) % 4


def place(buffer, block, *index):
    start = tuple(index) + (0,) * (buffer.ndim - len(index))
    shape = (1,) * (buffer.ndim - block.ndim) + block.shape
    return lax.dynamic_update_slice(buffer, block.reshape(shape), start)


def halves(block):
    return block.reshape((2, -1) + block.shape[1:])


def put_kernel(sources, aliased, places, *refs):
    pieces, result = refs[aliased:-1], refs[-1]
    rows = result.shape[1]
    step = pl.program_id(0)
    for i, (piece, block) in enumerate(sources):

        @pl.when(step == i)
        def _():
            result[0] = pieces[piece][block * rows : (block + 1) * rows]


def put(buffer, pieces, sources, places, blocks, rows, vmem_limit=13 << 20):
    columns = pieces[0].shape[1]
    aliased = 0 if buffer is None else 1
    held = () if buffer is None else (buffer,)
    return pl.pallas_call(
        functools.partial(put_kernel, sources, aliased),
        grid_spec=pltpu.PrefetchScalarGridSpec(
            num_scalar_prefetch=1,
            grid=(len(sources),),
            in_specs=[pl.BlockSpec(memory_space=pl.ANY)] * aliased
            + [pl.BlockSpec(piece.shape, lambda i, *_: (0, 0)) for piece in pieces],
            out_specs=pl.BlockSpec((1, rows, columns), lambda i, places: (places[i], 0, 0)),
        ),
        out_shape=jax.ShapeDtypeStruct((blocks, rows, columns), pieces[0].dtype),
        input_output_aliases={1: 0} if aliased else {},
        compiler_params=pltpu.CompilerParams(vmem_limit_bytes=vmem_limit),
        cost_estimate=pl.CostEstimate(flops=0, bytes_accessed=rows, transcendentals=0),
        name="put",
    )(places, *held, *pieces)


def order_kernel(sources, places, *refs):
    pieces, result = refs[:-1], refs[-1]
    rows = result.shape[1]
    for i, (piece, block) in enumerate(sources):
        result[places[i]] = pieces[piece][block * rows : (block + 1) * rows]


def order(pieces, sources, places, blocks, rows):
    columns = pieces[0].shape[1]
    vmem = pl.BlockSpec(memory_space=pltpu.VMEM)
    return pl.pallas_call(
        functools.partial(order_kernel, sources),
        grid_spec=pltpu.PrefetchScalarGridSpec(
            num_scalar_prefetch=1, in_specs=[vmem] * len(pieces), out_specs=vmem
        ),
        out_shape=jax.ShapeDtypeStruct((blocks, rows, columns), pieces[0].dtype),
        compiler_params=pltpu.CompilerParams(vmem_limit_bytes=8 << 20),
        cost_estimate=pl.CostEstimate(flops=0, bytes_accessed=rows, transcendentals=0),
        name="order",
    )(places, *pieces)


def pack_kernel(payloads, pieces, *refs):
    for payload, out in zip(payloads, refs[pieces:]):
        start = 0
        for piece, source, count in payload:
            out[start : start + count] = refs[piece][source : source + count]
            start += count


def pack(pieces, payloads, steps, vmem_limit=8 << 20):
    columns = pieces[0].shape[1]
    rows = [sum(count for _, _, count in payload) for payload in payloads]
    block = lambda count: pl.BlockSpec((count, columns // steps), lambda i: (0, i))
    return pl.pallas_call(
        functools.partial(pack_kernel, tuple(payloads), len(pieces)),
        grid=(steps,),
        in_specs=[block(piece.shape[0]) for piece in pieces],
        out_specs=[block(count) for count in rows],
        out_shape=[jax.ShapeDtypeStruct((count, columns), pieces[0].dtype) for count in rows],
        compiler_params=pltpu.CompilerParams(vmem_limit_bytes=vmem_limit),
        cost_estimate=pl.CostEstimate(flops=0, bytes_accessed=sum(rows), transcendentals=0),
        name="pack",
    )(*pieces)


def shards(
    tokens,
    ln_gain,
    w_qkv,
    q_gain,
    k_gain,
    stored_keys,
    stored_values,
    span_lengths,
    fill_positions,
    w_out,
):
    barrier = lax.optimization_barrier
    wide, narrow = Ring("wide"), Ring("narrow")
    wide_count = lax.axis_size("wide")
    streams = span_lengths.shape[0]
    rows = tokens.shape[0] // lax.axis_size("narrow")
    slots = rows // streams
    depth = w_qkv.shape[0]
    half_rows, half_depth = rows // 2, depth // 2

    own_rows = lax.all_to_all(tokens, "narrow", split_axis=0, concat_axis=1, tiled=True)
    w_up, w_down, w_swap = narrow.up(w_qkv), narrow.down(w_qkv), narrow.swap(w_qkv)
    o_up, o_down = wide.up(w_out), wide.down(w_out)
    token_values = own_rows.astype(jnp.float32)
    own_squares = jnp.sum(token_values * token_values, axis=1)
    normed = (token_values * ln_gain[None, :]).astype(jnp.bfloat16)
    o_up, o_down, w_swap, w_up, w_down, normed = barrier(
        (o_up, o_down, w_swap, w_up, w_down, normed)
    )

    w_swap_up, w_swap_down = narrow.up(w_swap), narrow.down(w_swap)
    t_up, t_down, t_swap = wide.up(normed), wide.down(normed), wide.swap(normed)
    inverse = jnp.broadcast_to(lax.rsqrt(own_squares / D + EPSILON)[:, None], (rows, HEAD_SIZE))
    cosine, sine = turn_tables(fill_positions, slots)
    one, other = wide.at_pair, 1 - wide.at_pair
    every = jnp.zeros((2, 4, 2, 2, half_rows) + normed.shape[1:], normed.dtype)
    every = place(every, halves(normed), one, wide.ring(0), wide.at_core)
    w_swap_up, w_swap_down, t_up, t_down, t_swap, inverse, cosine, sine, every = barrier(
        (w_swap_up, w_swap_down, t_up, t_down, t_swap, inverse, cosine, sine, every)
    )

    w_far_up = narrow.up(jnp.concatenate([w_up[:half_depth], w_swap_up[:half_depth]]))
    w_far_down = narrow.down(jnp.concatenate([w_down[half_depth:], w_swap_down[half_depth:]]))
    t_two_up = wide.up(jnp.concatenate([t_swap, t_up[:half_rows]]))
    t_two_down = wide.down(jnp.concatenate([t_swap, t_down[half_rows:]]))
    o_swap = wide.swap(w_out)
    near = jnp.stack([normed, t_up, t_down, t_swap])
    at_narrow = tuple(
        narrow.ring(ring) * 2 + pair
        for pair in (narrow.at_pair, 1 - narrow.at_pair)
        for ring in (0, 3, 1, 2)
    )
    columns = put(
        None,
        (w_qkv, w_up, w_down, w_swap, w_swap_up, w_swap_down),
        tuple((i, half) for i in range(6) for half in range(2)),
        jnp.stack([at_narrow[i] * 2 + half for i in (0, 1, 2, 4, 5, 6) for half in range(2)]),
        16,
        half_depth,
    )
    every = place(every, halves(t_up), one, wide.ring(3), wide.at_core)
    every = place(every, halves(t_down), one, wide.ring(1), wide.at_core)
    every = place(every, halves(t_swap), other, wide.ring(0), wide.at_core)
    w_far_up, w_far_down, t_two_up, t_two_down, o_swap, near, columns, every = barrier(
        (w_far_up, w_far_down, t_two_up, t_two_down, o_swap, near, columns, every)
    )

    t_far_up = wide.up(t_two_up[:half_rows])
    t_far_down = wide.down(t_two_down[half_rows:rows])
    near = wide.cores(near)
    two = wide.cores(jnp.stack([t_two_up, t_two_down]))
    far = wide.cores(jnp.stack([t_far_up, t_far_down]))
    columns = put(
        columns,
        (w_far_up, w_far_down),
        ((0, 0), (1, 0), (0, 1), (1, 1)),
        jnp.stack([at_narrow[i] * 2 + half for i in (3, 7) for half in range(2)]),
        16,
        half_depth,
    ).reshape(-1, w_qkv.shape[1])
    for core, (two_up, two_down), (far_up, far_down) in (
        (wide.at_core, (t_two_up, t_two_down), (t_far_up, t_far_down)),
        (1 - wide.at_core, two, far),
    ):
        every = place(every, halves(two_up[:rows]), other, wide.ring(3), core)
        every = place(every, halves(two_down[:rows]), other, wide.ring(1), core)
        every = place(every, two_up[rows:], one, wide.ring(2), core, 0)
        every = place(every, two_down[rows:], one, wide.ring(2), core, 1)
        every = place(every, far_up, other, wide.ring(2), core, 0)
        every = place(every, far_down, other, wide.ring(2), core, 1)
    for block, pair, ring in zip(near, (one, one, one, other), (0, 3, 1, 0)):
        every = place(every, halves(block), pair, wide.ring(ring), 1 - wide.at_core)
    every = every.reshape(-1, normed.shape[1])
    every, columns = barrier((every, columns))
    projected = jnp.dot(every, columns, preferred_element_type=jnp.float32).astype(jnp.bfloat16)
    packed = lax.all_to_all(
        projected.reshape(wide_count, rows, -1), "wide", split_axis=0, concat_axis=0, tiled=True
    )
    packed, o_swap, o_up, o_down = barrier((packed, o_swap, o_up, o_down))

    out_rows = w_out.shape[0]
    half_out = out_rows // 2
    o_two_up = wide.up(jnp.concatenate([o_swap, o_up[:half_out]]))
    o_two_down = wide.down(jnp.concatenate([o_swap, o_down[half_out:]]))
    attended = attend(
        packed,
        inverse,
        cosine,
        sine,
        q_gain,
        k_gain,
        stored_keys,
        stored_values,
        span_lengths,
        fill_positions,
    )

    quarter = rows // 4
    attended, w_out, o_up, o_down, o_swap = barrier((attended, w_out, o_up, o_down, o_swap))
    a_up, a_down, a_swap = narrow.up(attended), narrow.down(attended), narrow.swap(attended)
    o_far_up = wide.up(o_two_up[:half_out])
    o_far_down = wide.down(o_two_down[half_out:out_rows])
    (o_near,) = pack(
        (w_out, o_up, o_down, o_swap, o_two_up, o_two_down),
        (
            tuple((i, 0, out_rows) for i in range(4))
            + tuple((i, 0, 3 * half_out) for i in (4, 5)),
        ),
        5,
        6 << 20,
    )
    other_far = jnp.stack([o_far_up, o_far_down])
    a_up, a_down, a_swap, o_far_up, o_far_down, o_near, other_far = barrier(
        (a_up, a_down, a_swap, o_far_up, o_far_down, o_near, other_far)
    )

    b_up = narrow.up(jnp.concatenate([a_swap[half_rows:], a_up[:half_rows]]))
    b_down = narrow.down(jnp.concatenate([a_swap[half_rows:], a_down[half_rows:]]))
    b_swap = narrow.swap(jnp.concatenate([a_up[:half_rows], a_down[:half_rows]]))
    o_near = wide.cores(o_near)
    other_far = wide.cores(other_far).reshape(out_rows, -1)
    chips = tuple(
        (pair * 4 + wide.ring(ring)) * 2
        for ring, pair in (
            (0, wide.at_pair),
            (3, wide.at_pair),
            (1, wide.at_pair),
            (0, 1 - wide.at_pair),
            (3, 1 - wide.at_pair),
            (1, 1 - wide.at_pair),
            (2, wide.at_pair),
            (2, 1 - wide.at_pair),
        )
    )
    every_w_out = put(
        None,
        (w_out, o_up, o_down, o_swap, o_two_up, o_two_down, o_far_up, o_far_down),
        tuple((i, half) for i in range(6) for half in range(2))
        + ((4, 2), (5, 2), (6, 0), (7, 0)),
        jnp.stack([(chip + wide.at_core) * 2 + half for chip in chips for half in range(2)]),
        wide_count * 2,
        half_out,
    )
    every_w_out = put(
        every_w_out,
        (o_near, other_far),
        tuple((0, i) for i in (0, 1, 2, 3, 4, 5, 6, 7, 8, 9, 11, 12, 10, 13)) + ((1, 0), (1, 1)),
        jnp.stack([(chip + 1 - wide.at_core) * 2 + half for chip in chips for half in range(2)]),
        wide_count * 2,
        half_out,
    ).reshape(-1, w_out.shape[1])

    def project_out(part):
        product = jnp.dot(part, every_w_out, preferred_element_type=jnp.float32)
        return product.astype(jnp.bfloat16)

    near_rows = project_out(jnp.concatenate([attended, a_swap, a_up, a_down]))
    b_up, b_down, b_swap, near_rows = barrier((b_up, b_down, b_swap, near_rows))
    c_up = narrow.up(b_up[:quarter])
    c_down = narrow.down(b_down[quarter:half_rows])
    c_swap = narrow.swap(b_up[half_rows : half_rows + quarter])
    c_swap_last = narrow.swap(b_up[half_rows + quarter :])
    one, other = narrow.at_pair, 1 - narrow.at_pair
    place_of = lambda ring, pair, half: (narrow.ring(ring) * 2 + pair) * 2 + half
    result = order(
        (near_rows, project_out(jnp.concatenate([b_swap, b_up, b_down]))),
        tuple((0, i) for i in range(8)) + tuple((1, i) for i in range(6)),
        jnp.stack(
            [
                place_of(ring, pair, half)
                for ring, pair in ((0, one), (0, other), (3, one), (1, one))
                for half in range(2)
            ]
            + [
                place_of(*place)
                for place in (
                    (3, other, 0),
                    (1, other, 0),
                    (3, other, 1),
                    (2, one, 0),
                    (1, other, 1),
                    (2, one, 1),
                )
            ]
        ),
        16,
        half_rows,
    )
    c_up, c_down, c_swap, c_swap_last, result = barrier(
        (c_up, c_down, c_swap, c_swap_last, result)
    )
    result = put(
        result,
        (project_out(jnp.concatenate([c_swap, c_swap_last, c_up, c_down])),),
        ((0, 0), (0, 1)),
        jnp.stack([place_of(2, other, 0), place_of(2, other, 1)]),
        16,
        half_rows,
    )
    return result.reshape(-1, result.shape[-1])


def solution(mesh):
    placed = (
        P("wide", "narrow"),
        P(),
        P("narrow", "wide"),
        P(),
        P(),
        P(("wide", "narrow"), None, None),
        P(("wide", "narrow"), None, None),
        P(("wide", "narrow")),
        P(("wide", "narrow")),
        P("wide", "narrow"),
    )
    return jax.shard_map(
        shards, mesh=mesh, in_specs=placed, out_specs=P("wide", "narrow"), check_vma=False
    )
```

```python
import functools
import math

import jax
import jax.numpy as jnp
from jax import lax
from jax.experimental import pallas as pl
from jax.experimental.pallas import tpu as pltpu
from jax.sharding import PartitionSpec as P

D = 5120
QUERY_HEADS = 64
KEY_VALUE_HEADS = 8
HEAD_SIZE = 128


EPSILON = 1e-06
ROPE_BASE = 1000000.0


def turn_tables(fill_positions, slots):
    half = HEAD_SIZE // 2
    slot_index = jnp.arange(slots, dtype=jnp.int32)
    position = (fill_positions[:, None] + slot_index[None, :]).reshape(-1).astype(jnp.float32)
    frequency = jnp.exp(
        jnp.arange(half, dtype=jnp.float32) * (-2.0 * math.log(ROPE_BASE) / HEAD_SIZE)
    )
    angles = position[:, None] * frequency[None, :]
    cosine, sine = jnp.cos(angles), jnp.sin(angles)
    return (
        jnp.concatenate([cosine, cosine], axis=1),
        jnp.concatenate([-sine, sine], axis=1),
    )


def attend_kernel(
    fills,
    spans,
    packed,
    inverse,
    cosine,
    sine,
    q_gain,
    k_gain,
    keys,
    values,
    attended,
):
    stream = pl.program_id(0)
    fill, span = fills[stream], spans[stream]
    slots = packed.shape[1]
    frames = keys.shape[1]
    group = QUERY_HEADS // KEY_VALUE_HEADS
    rows = group * slots
    cos_one, sin_one = cosine[...], sine[...]

    def turned(vectors, gains, cos_rows, sin_rows):
        mean_square = jnp.mean(vectors * vectors, axis=-1, keepdims=True)
        normed = vectors * lax.rsqrt(mean_square + EPSILON) * gains
        swapped = pltpu.roll(normed, HEAD_SIZE // 2, 1)
        return (normed * cos_rows + swapped * sin_rows).astype(jnp.bfloat16)

    cos_all = jnp.concatenate([cos_one] * group, axis=0)
    sin_all = jnp.concatenate([sin_one] * group, axis=0)
    low = lax.broadcasted_iota(jnp.int32, (slots, HEAD_SIZE), 1) < HEAD_SIZE // 2
    frame_live = lax.broadcasted_iota(jnp.int32, (rows, frames), 1) < fill
    slot_row = lax.broadcasted_iota(jnp.int32, (group, slots, HEAD_SIZE), 1)
    slot_row = slot_row.reshape(rows, HEAD_SIZE)
    slot_column = lax.broadcasted_iota(jnp.int32, (rows, HEAD_SIZE), 1)
    slot_live = (slot_column <= slot_row) & (slot_column < span)
    row_live = slot_row < span
    empty = jnp.zeros((HEAD_SIZE - slots, HEAD_SIZE), jnp.bfloat16)
    query_columns = group // 2 * HEAD_SIZE
    contract_last = (((1,), (1,)), ((), ()))
    exp_scale = math.log2(math.e) / math.sqrt(HEAD_SIZE)
    def prepare(head):
        queries = jnp.concatenate(
            [
                packed[2 * head + g // 4, :, g % 4 * HEAD_SIZE : (g % 4 + 1) * HEAD_SIZE]
                for g in range(group)
            ],
            axis=0,
        ).astype(jnp.float32)
        queries = turned(queries, q_gain[...], cos_all, sin_all)
        first = packed[2 * head, :, query_columns:].astype(jnp.float32)
        second = packed[2 * head + 1, :, query_columns:].astype(jnp.float32)
        fresh_key = jnp.where(low, first, pltpu.roll(second, HEAD_SIZE // 2, 1))
        fresh_value = jnp.where(low, pltpu.roll(first, HEAD_SIZE // 2, 1), second)
        fresh_key = jnp.concatenate([turned(fresh_key, k_gain[...], cos_one, sin_one), empty])
        fresh_value = jnp.concatenate([(fresh_value * inverse[...]).astype(jnp.bfloat16), empty])
        return queries, fresh_key, fresh_value

    def score(head, queries, fresh_key):
        columns = slice(head * HEAD_SIZE, (head + 1) * HEAD_SIZE)
        old = lax.dot_general(
            queries, keys[0, :, columns], contract_last, preferred_element_type=jnp.float32
        )
        new = lax.dot_general(
            queries, fresh_key, contract_last, preferred_element_type=jnp.float32
        )
        return old, new

    def weigh(old, new):
        old = jnp.where(frame_live, old, -1e30)
        new = jnp.where(slot_live, new, -1e30)
        scores = jnp.concatenate([old, new], axis=1)
        weights = jnp.exp2((scores - jnp.max(scores, axis=-1, keepdims=True)) * exp_scale)
        return weights.astype(jnp.bfloat16), jnp.sum(weights, axis=-1, keepdims=True)

    def mix(head, weights, total, fresh_value):
        columns = slice(head * HEAD_SIZE, (head + 1) * HEAD_SIZE)
        mixed = jnp.dot(
            weights[:, :frames], values[0, :, columns], preferred_element_type=jnp.float32
        ) + jnp.dot(weights[:, frames:], fresh_value, preferred_element_type=jnp.float32)
        mixed = jnp.where(row_live, mixed / total, 0.0).astype(jnp.bfloat16)
        for g in range(group):
            start = (head * group + g) * HEAD_SIZE
            attended[:, start : start + HEAD_SIZE] = mixed[g * slots : (g + 1) * slots]

    for pair in range(0, KEY_VALUE_HEADS, 2):
        heads = (pair, pair + 1)
        prepared = [prepare(head) for head in heads]
        scored = [score(head, p[0], p[1]) for head, p in zip(heads, prepared)]
        weighed = [weigh(*s) for s in scored]
        for head, w, p in zip(heads, weighed, prepared):
            mix(head, *w, p[2])


def attend(packed, inverse, cosine, sine, q_gain, k_gain, keys, values, spans, fills):
    groups, rows, columns = packed.shape
    streams, frames, width = keys.shape
    slots = rows // streams
    heads = QUERY_HEADS * HEAD_SIZE
    tables = pl.BlockSpec((slots, HEAD_SIZE), lambda s, *_: (s, 0))
    gains = pl.BlockSpec((1, HEAD_SIZE), lambda s, *_: (0, 0))
    cache = pl.BlockSpec((1, frames, width), lambda s, *_: (s, 0, 0))
    return pl.pallas_call(
        attend_kernel,
        grid_spec=pltpu.PrefetchScalarGridSpec(
            num_scalar_prefetch=2,
            grid=(streams,),
            in_specs=[
                pl.BlockSpec((groups, slots, columns), lambda s, *_: (0, s, 0)),
                tables,
                tables,
                tables,
                gains,
                gains,
                cache,
                cache,
            ],
            out_specs=pl.BlockSpec((slots, heads), lambda s, *_: (s, 0)),
        ),
        out_shape=jax.ShapeDtypeStruct((rows, heads), jnp.bfloat16),
        compiler_params=pltpu.CompilerParams(vmem_limit_bytes=24 << 20),
        cost_estimate=pl.CostEstimate(
            flops=4 * rows * heads * (frames + slots),
            bytes_accessed=4 * streams * frames * width + 4 * rows * 9216,
            transcendentals=rows * QUERY_HEADS * (frames + slots),
        ),
        name="attend",
    )(
        fills,
        spans,
        packed,
        inverse,
        cosine,
        sine,
        q_gain[None],
        k_gain[None],
        keys,
        values,
    )


class Ring:
    def __init__(self, axis):
        self.axis = axis
        if axis == "narrow":
            self.split = lambda i: (i // 2, i % 2, 0)
        else:
            self.split = lambda i: (i // 2 % 4, i // 8, i % 2)
        self.places = [self.split(i) for i in range(lax.axis_size(axis))]
        index_of = {place: i for i, place in enumerate(self.places)}

        def pairs(steps, flip, core):
            return [
                (i, index_of[((r + steps) % 4, p ^ flip, c ^ core)])
                for i, (r, p, c) in enumerate(self.places)
            ]

        self.pairs = pairs
        self.at_ring, self.at_pair, self.at_core = self.split(lax.axis_index(axis))

    def up(self, block):
        return lax.ppermute(block, self.axis, self.pairs(1, 0, 0))

    def down(self, block):
        return lax.ppermute(block, self.axis, self.pairs(-1, 0, 0))

    def swap(self, block):
        return lax.ppermute(block, self.axis, self.pairs(0, 1, 0))

    def cores(self, block):
        return lax.ppermute(block, self.axis, self.pairs(0, 0, 1))

    def ring(self, steps):
        return (self.at_ring + steps) % 4


def place(buffer, block, *index):
    start = tuple(index) + (0,) * (buffer.ndim - len(index))
    shape = (1,) * (buffer.ndim - block.ndim) + block.shape
    return lax.dynamic_update_slice(buffer, block.reshape(shape), start)


def halves(block):
    return block.reshape((2, -1) + block.shape[1:])


def put_kernel(sources, aliased, places, *refs):
    pieces, result = refs[aliased:-1], refs[-1]
    rows = result.shape[1]
    step = pl.program_id(0)
    for i, (piece, block) in enumerate(sources):

        @pl.when(step == i)
        def _():
            result[0] = pieces[piece][block * rows : (block + 1) * rows]


def put(buffer, pieces, sources, places, blocks, rows, vmem_limit=13 << 20):
    columns = pieces[0].shape[1]
    aliased = 0 if buffer is None else 1
    held = () if buffer is None else (buffer,)
    return pl.pallas_call(
        functools.partial(put_kernel, sources, aliased),
        grid_spec=pltpu.PrefetchScalarGridSpec(
            num_scalar_prefetch=1,
            grid=(len(sources),),
            in_specs=[pl.BlockSpec(memory_space=pl.ANY)] * aliased
            + [pl.BlockSpec(piece.shape, lambda i, *_: (0, 0)) for piece in pieces],
            out_specs=pl.BlockSpec((1, rows, columns), lambda i, places: (places[i], 0, 0)),
        ),
        out_shape=jax.ShapeDtypeStruct((blocks, rows, columns), pieces[0].dtype),
        input_output_aliases={1: 0} if aliased else {},
        compiler_params=pltpu.CompilerParams(vmem_limit_bytes=vmem_limit),
        cost_estimate=pl.CostEstimate(flops=0, bytes_accessed=rows, transcendentals=0),
        name="put",
    )(places, *held, *pieces)


def order_kernel(sources, places, *refs):
    pieces, result = refs[:-1], refs[-1]
    rows = result.shape[1]
    for i, (piece, block) in enumerate(sources):
        result[places[i]] = pieces[piece][block * rows : (block + 1) * rows]


def order(pieces, sources, places, blocks, rows):
    columns = pieces[0].shape[1]
    vmem = pl.BlockSpec(memory_space=pltpu.VMEM)
    return pl.pallas_call(
        functools.partial(order_kernel, sources),
        grid_spec=pltpu.PrefetchScalarGridSpec(
            num_scalar_prefetch=1, in_specs=[vmem] * len(pieces), out_specs=vmem
        ),
        out_shape=jax.ShapeDtypeStruct((blocks, rows, columns), pieces[0].dtype),
        compiler_params=pltpu.CompilerParams(vmem_limit_bytes=8 << 20),
        cost_estimate=pl.CostEstimate(flops=0, bytes_accessed=rows, transcendentals=0),
        name="order",
    )(places, *pieces)


def pack_kernel(payloads, pieces, *refs):
    for payload, out in zip(payloads, refs[pieces:]):
        start = 0
        for piece, source, count in payload:
            out[start : start + count] = refs[piece][source : source + count]
            start += count


def pack(pieces, payloads, steps, vmem_limit=8 << 20):
    columns = pieces[0].shape[1]
    rows = [sum(count for _, _, count in payload) for payload in payloads]
    block = lambda count: pl.BlockSpec((count, columns // steps), lambda i: (0, i))
    return pl.pallas_call(
        functools.partial(pack_kernel, tuple(payloads), len(pieces)),
        grid=(steps,),
        in_specs=[block(piece.shape[0]) for piece in pieces],
        out_specs=[block(count) for count in rows],
        out_shape=[jax.ShapeDtypeStruct((count, columns), pieces[0].dtype) for count in rows],
        compiler_params=pltpu.CompilerParams(vmem_limit_bytes=vmem_limit),
        cost_estimate=pl.CostEstimate(flops=0, bytes_accessed=sum(rows), transcendentals=0),
        name="pack",
    )(*pieces)


def shards(
    tokens,
    ln_gain,
    w_qkv,
    q_gain,
    k_gain,
    stored_keys,
    stored_values,
    span_lengths,
    fill_positions,
    w_out,
):
    barrier = lax.optimization_barrier
    wide, narrow = Ring("wide"), Ring("narrow")
    wide_count = lax.axis_size("wide")
    streams = span_lengths.shape[0]
    rows = tokens.shape[0] // lax.axis_size("narrow")
    slots = rows // streams
    depth = w_qkv.shape[0]
    half_rows, half_depth = rows // 2, depth // 2

    own_rows = lax.all_to_all(tokens, "narrow", split_axis=0, concat_axis=1, tiled=True)
    w_up, w_down, w_swap = narrow.up(w_qkv), narrow.down(w_qkv), narrow.swap(w_qkv)
    o_up, o_down = wide.up(w_out), wide.down(w_out)
    token_values = own_rows.astype(jnp.float32)
    own_squares = jnp.sum(token_values * token_values, axis=1)
    normed = (token_values * ln_gain[None, :]).astype(jnp.bfloat16)
    o_up, o_down, w_swap, w_up, w_down, normed = barrier(
        (o_up, o_down, w_swap, w_up, w_down, normed)
    )

    w_swap_up, w_swap_down = narrow.up(w_swap), narrow.down(w_swap)
    t_up, t_down, t_swap = wide.up(normed), wide.down(normed), wide.swap(normed)
    inverse = jnp.broadcast_to(lax.rsqrt(own_squares / D + EPSILON)[:, None], (rows, HEAD_SIZE))
    cosine, sine = turn_tables(fill_positions, slots)
    one, other = wide.at_pair, 1 - wide.at_pair
    every = jnp.zeros((2, 4, 2, 2, half_rows) + normed.shape[1:], normed.dtype)
    every = place(every, halves(normed), one, wide.ring(0), wide.at_core)
    w_swap_up, w_swap_down, t_up, t_down, t_swap, inverse, cosine, sine, every = barrier(
        (w_swap_up, w_swap_down, t_up, t_down, t_swap, inverse, cosine, sine, every)
    )

    w_far_up = narrow.up(jnp.concatenate([w_up[:half_depth], w_swap_up[:half_depth]]))
    w_far_down = narrow.down(jnp.concatenate([w_down[half_depth:], w_swap_down[half_depth:]]))
    t_two_up = wide.up(jnp.concatenate([t_swap, t_up[:half_rows]]))
    t_two_down = wide.down(jnp.concatenate([t_swap, t_down[half_rows:]]))
    o_swap = wide.swap(w_out)
    near = jnp.stack([normed, t_up, t_down, t_swap])
    at_narrow = tuple(
        narrow.ring(ring) * 2 + pair
        for pair in (narrow.at_pair, 1 - narrow.at_pair)
        for ring in (0, 3, 1, 2)
    )
    columns = put(
        None,
        (w_qkv, w_up, w_down, w_swap, w_swap_up, w_swap_down),
        tuple((i, half) for i in range(6) for half in range(2)),
        jnp.stack([at_narrow[i] * 2 + half for i in (0, 1, 2, 4, 5, 6) for half in range(2)]),
        16,
        half_depth,
    )
    every = place(every, halves(t_up), one, wide.ring(3), wide.at_core)
    every = place(every, halves(t_down), one, wide.ring(1), wide.at_core)
    every = place(every, halves(t_swap), other, wide.ring(0), wide.at_core)
    w_far_up, w_far_down, t_two_up, t_two_down, o_swap, near, columns, every = barrier(
        (w_far_up, w_far_down, t_two_up, t_two_down, o_swap, near, columns, every)
    )

    t_far_up = wide.up(t_two_up[:half_rows])
    t_far_down = wide.down(t_two_down[half_rows:rows])
    near = wide.cores(near)
    two = wide.cores(jnp.stack([t_two_up, t_two_down]))
    far = wide.cores(jnp.stack([t_far_up, t_far_down]))
    columns = put(
        columns,
        (w_far_up, w_far_down),
        ((0, 0), (1, 0), (0, 1), (1, 1)),
        jnp.stack([at_narrow[i] * 2 + half for i in (3, 7) for half in range(2)]),
        16,
        half_depth,
    ).reshape(-1, w_qkv.shape[1])
    for core, (two_up, two_down), (far_up, far_down) in (
        (wide.at_core, (t_two_up, t_two_down), (t_far_up, t_far_down)),
        (1 - wide.at_core, two, far),
    ):
        every = place(every, halves(two_up[:rows]), other, wide.ring(3), core)
        every = place(every, halves(two_down[:rows]), other, wide.ring(1), core)
        every = place(every, two_up[rows:], one, wide.ring(2), core, 0)
        every = place(every, two_down[rows:], one, wide.ring(2), core, 1)
        every = place(every, far_up, other, wide.ring(2), core, 0)
        every = place(every, far_down, other, wide.ring(2), core, 1)
    for block, pair, ring in zip(near, (one, one, one, other), (0, 3, 1, 0)):
        every = place(every, halves(block), pair, wide.ring(ring), 1 - wide.at_core)
    every = every.reshape(-1, normed.shape[1])
    every, columns = barrier((every, columns))
    projected = jnp.dot(every, columns, preferred_element_type=jnp.float32).astype(jnp.bfloat16)
    packed = lax.all_to_all(
        projected.reshape(wide_count, rows, -1), "wide", split_axis=0, concat_axis=0, tiled=True
    )
    packed, o_swap, o_up, o_down = barrier((packed, o_swap, o_up, o_down))

    out_rows = w_out.shape[0]
    half_out = out_rows // 2
    o_two_up = wide.up(jnp.concatenate([o_swap, o_up[:half_out]]))
    o_two_down = wide.down(jnp.concatenate([o_swap, o_down[half_out:]]))
    attended = attend(
        packed,
        inverse,
        cosine,
        sine,
        q_gain,
        k_gain,
        stored_keys,
        stored_values,
        span_lengths,
        fill_positions,
    )

    quarter = rows // 4
    attended, w_out, o_up, o_down, o_swap = barrier((attended, w_out, o_up, o_down, o_swap))
    a_up, a_down, a_swap = narrow.up(attended), narrow.down(attended), narrow.swap(attended)
    o_far_up = wide.up(o_two_up[:half_out])
    o_far_down = wide.down(o_two_down[half_out:out_rows])
    (o_near,) = pack(
        (w_out, o_up, o_down, o_swap, o_two_up, o_two_down),
        (
            tuple((i, 0, out_rows) for i in range(4))
            + tuple((i, 0, 3 * half_out) for i in (4, 5)),
        ),
        5,
        6 << 20,
    )
    other_far = jnp.stack([o_far_up, o_far_down])
    a_up, a_down, a_swap, o_far_up, o_far_down, o_near, other_far = barrier(
        (a_up, a_down, a_swap, o_far_up, o_far_down, o_near, other_far)
    )

    b_up = narrow.up(jnp.concatenate([a_swap[half_rows:], a_up[:half_rows]]))
    b_down = narrow.down(jnp.concatenate([a_swap[half_rows:], a_down[half_rows:]]))
    b_swap = narrow.swap(jnp.concatenate([a_up[:half_rows], a_down[:half_rows]]))
    o_near = wide.cores(o_near)
    other_far = wide.cores(other_far).reshape(out_rows, -1)
    near_rows = jnp.concatenate([attended, a_swap, a_up, a_down])
    near_rows, o_near, other_far = barrier((near_rows, o_near, other_far))
    chips = tuple(
        (pair * 4 + wide.ring(ring)) * 2
        for ring, pair in (
            (0, wide.at_pair),
            (3, wide.at_pair),
            (1, wide.at_pair),
            (0, 1 - wide.at_pair),
            (3, 1 - wide.at_pair),
            (1, 1 - wide.at_pair),
            (2, wide.at_pair),
            (2, 1 - wide.at_pair),
        )
    )
    every_w_out = put(
        None,
        (w_out, o_up, o_down, o_swap, o_two_up, o_two_down, o_far_up, o_far_down),
        tuple((i, half) for i in range(6) for half in range(2))
        + ((4, 2), (5, 2), (6, 0), (7, 0)),
        jnp.stack([(chip + wide.at_core) * 2 + half for chip in chips for half in range(2)]),
        wide_count * 2,
        half_out,
    )
    every_w_out = put(
        every_w_out,
        (o_near, other_far),
        tuple((0, i) for i in (0, 1, 2, 3, 4, 5, 6, 7, 8, 9, 11, 12, 10, 13)) + ((1, 0), (1, 1)),
        jnp.stack([(chip + 1 - wide.at_core) * 2 + half for chip in chips for half in range(2)]),
        wide_count * 2,
        half_out,
    ).reshape(-1, w_out.shape[1])

    def project_out(part):
        product = jnp.dot(part, every_w_out, preferred_element_type=jnp.float32)
        return product.astype(jnp.bfloat16)

    near_rows = project_out(near_rows)
    b_up, b_down, b_swap, near_rows = barrier((b_up, b_down, b_swap, near_rows))
    c_up = narrow.up(b_up[:quarter])
    c_down = narrow.down(b_down[quarter:half_rows])
    c_swap = narrow.swap(b_up[half_rows : half_rows + quarter])
    c_swap_last = narrow.swap(b_up[half_rows + quarter :])
    one, other = narrow.at_pair, 1 - narrow.at_pair
    place_of = lambda ring, pair, half: (narrow.ring(ring) * 2 + pair) * 2 + half
    result = order(
        (near_rows, project_out(jnp.concatenate([b_swap, b_up, b_down]))),
        tuple((0, i) for i in range(8)) + tuple((1, i) for i in range(6)),
        jnp.stack(
            [
                place_of(ring, pair, half)
                for ring, pair in ((0, one), (0, other), (3, one), (1, one))
                for half in range(2)
            ]
            + [
                place_of(*place)
                for place in (
                    (3, other, 0),
                    (1, other, 0),
                    (3, other, 1),
                    (2, one, 0),
                    (1, other, 1),
                    (2, one, 1),
                )
            ]
        ),
        16,
        half_rows,
    )
    c_up, c_down, c_swap, c_swap_last, result = barrier(
        (c_up, c_down, c_swap, c_swap_last, result)
    )
    result = put(
        result,
        (project_out(jnp.concatenate([c_swap, c_swap_last, c_up, c_down])),),
        ((0, 0), (0, 1)),
        jnp.stack([place_of(2, other, 0), place_of(2, other, 1)]),
        16,
        half_rows,
    )
    return result.reshape(-1, result.shape[-1])


def solution(mesh):
    placed = (
        P("wide", "narrow"),
        P(),
        P("narrow", "wide"),
        P(),
        P(),
        P(("wide", "narrow"), None, None),
        P(("wide", "narrow"), None, None),
        P(("wide", "narrow")),
        P(("wide", "narrow")),
        P("wide", "narrow"),
    )
    return jax.shard_map(
        shards, mesh=mesh, in_specs=placed, out_specs=P("wide", "narrow"), check_vma=False
    )
```

```python
import functools
import math

import jax
import jax.numpy as jnp
from jax import lax
from jax.experimental import pallas as pl
from jax.experimental.pallas import tpu as pltpu
from jax.sharding import PartitionSpec as P

D = 5120
QUERY_HEADS = 64
KEY_VALUE_HEADS = 8
HEAD_SIZE = 128


EPSILON = 1e-06
ROPE_BASE = 1000000.0


def turn_tables(fill_positions, slots):
    half = HEAD_SIZE // 2
    slot_index = jnp.arange(slots, dtype=jnp.int32)
    position = (fill_positions[:, None] + slot_index[None, :]).reshape(-1).astype(jnp.float32)
    frequency = jnp.exp(
        jnp.arange(half, dtype=jnp.float32) * (-2.0 * math.log(ROPE_BASE) / HEAD_SIZE)
    )
    angles = position[:, None] * frequency[None, :]
    cosine, sine = jnp.cos(angles), jnp.sin(angles)
    return (
        jnp.concatenate([cosine, cosine], axis=1),
        jnp.concatenate([-sine, sine], axis=1),
    )


def attend_kernel(
    fills,
    spans,
    packed,
    inverse,
    cosine,
    sine,
    q_gain,
    k_gain,
    keys,
    values,
    attended,
):
    stream = pl.program_id(0)
    fill, span = fills[stream], spans[stream]
    slots = packed.shape[1]
    frames = keys.shape[1]
    group = QUERY_HEADS // KEY_VALUE_HEADS
    rows = group * slots
    cos_one, sin_one = cosine[...], sine[...]

    def turned(vectors, gains, cos_rows, sin_rows):
        mean_square = jnp.mean(vectors * vectors, axis=-1, keepdims=True)
        normed = vectors * lax.rsqrt(mean_square + EPSILON) * gains
        swapped = pltpu.roll(normed, HEAD_SIZE // 2, 1)
        return (normed * cos_rows + swapped * sin_rows).astype(jnp.bfloat16)

    cos_all = jnp.concatenate([cos_one] * group, axis=0)
    sin_all = jnp.concatenate([sin_one] * group, axis=0)
    low = lax.broadcasted_iota(jnp.int32, (slots, HEAD_SIZE), 1) < HEAD_SIZE // 2
    frame_live = lax.broadcasted_iota(jnp.int32, (rows, frames), 1) < fill
    slot_row = lax.broadcasted_iota(jnp.int32, (group, slots, HEAD_SIZE), 1)
    slot_row = slot_row.reshape(rows, HEAD_SIZE)
    slot_column = lax.broadcasted_iota(jnp.int32, (rows, HEAD_SIZE), 1)
    slot_live = (slot_column <= slot_row) & (slot_column < span)
    row_live = slot_row < span
    empty = jnp.zeros((HEAD_SIZE - slots, HEAD_SIZE), jnp.bfloat16)
    query_columns = group // 2 * HEAD_SIZE
    contract_last = (((1,), (1,)), ((), ()))
    exp_scale = math.log2(math.e) / math.sqrt(HEAD_SIZE)
    def prepare(head):
        queries = jnp.concatenate(
            [
                packed[2 * head + g // 4, :, g % 4 * HEAD_SIZE : (g % 4 + 1) * HEAD_SIZE]
                for g in range(group)
            ],
            axis=0,
        ).astype(jnp.float32)
        queries = turned(queries, q_gain[...], cos_all, sin_all)
        first = packed[2 * head, :, query_columns:].astype(jnp.float32)
        second = packed[2 * head + 1, :, query_columns:].astype(jnp.float32)
        fresh_key = jnp.where(low, first, pltpu.roll(second, HEAD_SIZE // 2, 1))
        fresh_value = jnp.where(low, pltpu.roll(first, HEAD_SIZE // 2, 1), second)
        fresh_key = jnp.concatenate([turned(fresh_key, k_gain[...], cos_one, sin_one), empty])
        fresh_value = jnp.concatenate([(fresh_value * inverse[...]).astype(jnp.bfloat16), empty])
        return queries, fresh_key, fresh_value

    def score(head, queries, fresh_key):
        columns = slice(head * HEAD_SIZE, (head + 1) * HEAD_SIZE)
        old = lax.dot_general(
            queries, keys[0, :, columns], contract_last, preferred_element_type=jnp.float32
        )
        new = lax.dot_general(
            queries, fresh_key, contract_last, preferred_element_type=jnp.float32
        )
        return old, new

    def weigh(old, new):
        old = jnp.where(frame_live, old, -1e30)
        new = jnp.where(slot_live, new, -1e30)
        scores = jnp.concatenate([old, new], axis=1)
        weights = jnp.exp2((scores - jnp.max(scores, axis=-1, keepdims=True)) * exp_scale)
        return weights.astype(jnp.bfloat16), jnp.sum(weights, axis=-1, keepdims=True)

    def mix(head, weights, total, fresh_value):
        columns = slice(head * HEAD_SIZE, (head + 1) * HEAD_SIZE)
        mixed = jnp.dot(
            weights[:, :frames], values[0, :, columns], preferred_element_type=jnp.float32
        ) + jnp.dot(weights[:, frames:], fresh_value, preferred_element_type=jnp.float32)
        mixed = jnp.where(row_live, mixed / total, 0.0).astype(jnp.bfloat16)
        for g in range(group):
            start = (head * group + g) * HEAD_SIZE
            attended[:, start : start + HEAD_SIZE] = mixed[g * slots : (g + 1) * slots]

    for pair in range(0, KEY_VALUE_HEADS, 2):
        heads = (pair, pair + 1)
        prepared = [prepare(head) for head in heads]
        scored = [score(head, p[0], p[1]) for head, p in zip(heads, prepared)]
        weighed = [weigh(*s) for s in scored]
        for head, w, p in zip(heads, weighed, prepared):
            mix(head, *w, p[2])


def attend(packed, inverse, cosine, sine, q_gain, k_gain, keys, values, spans, fills):
    groups, rows, columns = packed.shape
    streams, frames, width = keys.shape
    slots = rows // streams
    heads = QUERY_HEADS * HEAD_SIZE
    tables = pl.BlockSpec((slots, HEAD_SIZE), lambda s, *_: (s, 0))
    gains = pl.BlockSpec((1, HEAD_SIZE), lambda s, *_: (0, 0))
    cache = pl.BlockSpec((1, frames, width), lambda s, *_: (s, 0, 0))
    return pl.pallas_call(
        attend_kernel,
        grid_spec=pltpu.PrefetchScalarGridSpec(
            num_scalar_prefetch=2,
            grid=(streams,),
            in_specs=[
                pl.BlockSpec((groups, slots, columns), lambda s, *_: (0, s, 0)),
                tables,
                tables,
                tables,
                gains,
                gains,
                cache,
                cache,
            ],
            out_specs=pl.BlockSpec((slots, heads), lambda s, *_: (s, 0)),
        ),
        out_shape=jax.ShapeDtypeStruct((rows, heads), jnp.bfloat16),
        compiler_params=pltpu.CompilerParams(vmem_limit_bytes=24 << 20),
        cost_estimate=pl.CostEstimate(
            flops=4 * rows * heads * (frames + slots),
            bytes_accessed=4 * streams * frames * width + 4 * rows * 9216,
            transcendentals=rows * QUERY_HEADS * (frames + slots),
        ),
        name="attend",
    )(
        fills,
        spans,
        packed,
        inverse,
        cosine,
        sine,
        q_gain[None],
        k_gain[None],
        keys,
        values,
    )


class Ring:
    def __init__(self, axis):
        self.axis = axis
        if axis == "narrow":
            self.split = lambda i: (i // 2, i % 2, 0)
        else:
            self.split = lambda i: (i // 2 % 4, i // 8, i % 2)
        self.places = [self.split(i) for i in range(lax.axis_size(axis))]
        index_of = {place: i for i, place in enumerate(self.places)}

        def pairs(steps, flip, core):
            return [
                (i, index_of[((r + steps) % 4, p ^ flip, c ^ core)])
                for i, (r, p, c) in enumerate(self.places)
            ]

        self.pairs = pairs
        self.at_ring, self.at_pair, self.at_core = self.split(lax.axis_index(axis))

    def up(self, block):
        return lax.ppermute(block, self.axis, self.pairs(1, 0, 0))

    def down(self, block):
        return lax.ppermute(block, self.axis, self.pairs(-1, 0, 0))

    def swap(self, block):
        return lax.ppermute(block, self.axis, self.pairs(0, 1, 0))

    def cores(self, block):
        return lax.ppermute(block, self.axis, self.pairs(0, 0, 1))

    def ring(self, steps):
        return (self.at_ring + steps) % 4


def place(buffer, block, *index):
    start = tuple(index) + (0,) * (buffer.ndim - len(index))
    shape = (1,) * (buffer.ndim - block.ndim) + block.shape
    return lax.dynamic_update_slice(buffer, block.reshape(shape), start)


def halves(block):
    return block.reshape((2, -1) + block.shape[1:])


def put_kernel(sources, aliased, places, *refs):
    pieces, result = refs[aliased:-1], refs[-1]
    rows = result.shape[1]
    step = pl.program_id(0)
    for i, (piece, block) in enumerate(sources):

        @pl.when(step == i)
        def _():
            result[0] = pieces[piece][block * rows : (block + 1) * rows]


def put(buffer, pieces, sources, places, blocks, rows, vmem_limit=13 << 20):
    columns = pieces[0].shape[1]
    aliased = 0 if buffer is None else 1
    held = () if buffer is None else (buffer,)
    return pl.pallas_call(
        functools.partial(put_kernel, sources, aliased),
        grid_spec=pltpu.PrefetchScalarGridSpec(
            num_scalar_prefetch=1,
            grid=(len(sources),),
            in_specs=[pl.BlockSpec(memory_space=pl.ANY)] * aliased
            + [pl.BlockSpec(piece.shape, lambda i, *_: (0, 0)) for piece in pieces],
            out_specs=pl.BlockSpec((1, rows, columns), lambda i, places: (places[i], 0, 0)),
        ),
        out_shape=jax.ShapeDtypeStruct((blocks, rows, columns), pieces[0].dtype),
        input_output_aliases={1: 0} if aliased else {},
        compiler_params=pltpu.CompilerParams(vmem_limit_bytes=vmem_limit),
        cost_estimate=pl.CostEstimate(flops=0, bytes_accessed=rows, transcendentals=0),
        name="put",
    )(places, *held, *pieces)


def order_kernel(sources, places, *refs):
    pieces, result = refs[:-1], refs[-1]
    rows = result.shape[1]
    for i, (piece, block) in enumerate(sources):
        result[places[i]] = pieces[piece][block * rows : (block + 1) * rows]


def order(pieces, sources, places, blocks, rows):
    columns = pieces[0].shape[1]
    vmem = pl.BlockSpec(memory_space=pltpu.VMEM)
    return pl.pallas_call(
        functools.partial(order_kernel, sources),
        grid_spec=pltpu.PrefetchScalarGridSpec(
            num_scalar_prefetch=1, in_specs=[vmem] * len(pieces), out_specs=vmem
        ),
        out_shape=jax.ShapeDtypeStruct((blocks, rows, columns), pieces[0].dtype),
        compiler_params=pltpu.CompilerParams(vmem_limit_bytes=8 << 20),
        cost_estimate=pl.CostEstimate(flops=0, bytes_accessed=rows, transcendentals=0),
        name="order",
    )(places, *pieces)


def pack_kernel(payloads, pieces, *refs):
    for payload, out in zip(payloads, refs[pieces:]):
        start = 0
        for piece, source, count in payload:
            out[start : start + count] = refs[piece][source : source + count]
            start += count


def pack(pieces, payloads, steps, vmem_limit=8 << 20):
    columns = pieces[0].shape[1]
    rows = [sum(count for _, _, count in payload) for payload in payloads]
    block = lambda count: pl.BlockSpec((count, columns // steps), lambda i: (0, i))
    return pl.pallas_call(
        functools.partial(pack_kernel, tuple(payloads), len(pieces)),
        grid=(steps,),
        in_specs=[block(piece.shape[0]) for piece in pieces],
        out_specs=[block(count) for count in rows],
        out_shape=[jax.ShapeDtypeStruct((count, columns), pieces[0].dtype) for count in rows],
        compiler_params=pltpu.CompilerParams(vmem_limit_bytes=vmem_limit),
        cost_estimate=pl.CostEstimate(flops=0, bytes_accessed=sum(rows), transcendentals=0),
        name="pack",
    )(*pieces)


def shards(
    tokens,
    ln_gain,
    w_qkv,
    q_gain,
    k_gain,
    stored_keys,
    stored_values,
    span_lengths,
    fill_positions,
    w_out,
):
    barrier = lax.optimization_barrier
    wide, narrow = Ring("wide"), Ring("narrow")
    wide_count = lax.axis_size("wide")
    streams = span_lengths.shape[0]
    rows = tokens.shape[0] // lax.axis_size("narrow")
    slots = rows // streams
    depth = w_qkv.shape[0]
    half_rows, half_depth = rows // 2, depth // 2

    own_rows = lax.all_to_all(tokens, "narrow", split_axis=0, concat_axis=1, tiled=True)
    w_up, w_down, w_swap = narrow.up(w_qkv), narrow.down(w_qkv), narrow.swap(w_qkv)
    o_up, o_down = wide.up(w_out), wide.down(w_out)
    token_values = own_rows.astype(jnp.float32)
    own_squares = jnp.sum(token_values * token_values, axis=1)
    normed = (token_values * ln_gain[None, :]).astype(jnp.bfloat16)
    o_up, o_down, w_swap, w_up, w_down, normed = barrier(
        (o_up, o_down, w_swap, w_up, w_down, normed)
    )

    w_swap_up, w_swap_down = narrow.up(w_swap), narrow.down(w_swap)
    t_up, t_down, t_swap = wide.up(normed), wide.down(normed), wide.swap(normed)
    inverse = jnp.broadcast_to(lax.rsqrt(own_squares / D + EPSILON)[:, None], (rows, HEAD_SIZE))
    cosine, sine = turn_tables(fill_positions, slots)
    one, other = wide.at_pair, 1 - wide.at_pair
    every = jnp.zeros((2, 4, 2, 2, half_rows) + normed.shape[1:], normed.dtype)
    every = place(every, halves(normed), one, wide.ring(0), wide.at_core)
    w_swap_up, w_swap_down, t_up, t_down, t_swap, inverse, cosine, sine, every = barrier(
        (w_swap_up, w_swap_down, t_up, t_down, t_swap, inverse, cosine, sine, every)
    )

    w_far_up = narrow.up(jnp.concatenate([w_up[:half_depth], w_swap_up[:half_depth]]))
    w_far_down = narrow.down(jnp.concatenate([w_down[half_depth:], w_swap_down[half_depth:]]))
    t_two_up = wide.up(jnp.concatenate([t_swap, t_up[:half_rows]]))
    t_two_down = wide.down(jnp.concatenate([t_swap, t_down[half_rows:]]))
    o_swap = wide.swap(w_out)
    near = jnp.stack([normed, t_up, t_down, t_swap])
    at_narrow = tuple(
        narrow.ring(ring) * 2 + pair
        for pair in (narrow.at_pair, 1 - narrow.at_pair)
        for ring in (0, 3, 1, 2)
    )
    columns = put(
        None,
        (w_qkv, w_up, w_down, w_swap, w_swap_up, w_swap_down),
        tuple((i, half) for i in range(6) for half in range(2)),
        jnp.stack([at_narrow[i] * 2 + half for i in (0, 1, 2, 4, 5, 6) for half in range(2)]),
        16,
        half_depth,
    )
    every = place(every, halves(t_up), one, wide.ring(3), wide.at_core)
    every = place(every, halves(t_down), one, wide.ring(1), wide.at_core)
    every = place(every, halves(t_swap), other, wide.ring(0), wide.at_core)
    w_far_up, w_far_down, t_two_up, t_two_down, o_swap, near, columns, every = barrier(
        (w_far_up, w_far_down, t_two_up, t_two_down, o_swap, near, columns, every)
    )

    t_far_up = wide.up(t_two_up[:half_rows])
    t_far_down = wide.down(t_two_down[half_rows:rows])
    near = wide.cores(near)
    two = wide.cores(jnp.stack([t_two_up, t_two_down]))
    far = wide.cores(jnp.stack([t_far_up, t_far_down]))
    columns = put(
        columns,
        (w_far_up, w_far_down),
        ((0, 0), (1, 0), (0, 1), (1, 1)),
        jnp.stack([at_narrow[i] * 2 + half for i in (3, 7) for half in range(2)]),
        16,
        half_depth,
    ).reshape(-1, w_qkv.shape[1])
    for core, (two_up, two_down), (far_up, far_down) in (
        (wide.at_core, (t_two_up, t_two_down), (t_far_up, t_far_down)),
        (1 - wide.at_core, two, far),
    ):
        every = place(every, halves(two_up[:rows]), other, wide.ring(3), core)
        every = place(every, halves(two_down[:rows]), other, wide.ring(1), core)
        every = place(every, two_up[rows:], one, wide.ring(2), core, 0)
        every = place(every, two_down[rows:], one, wide.ring(2), core, 1)
        every = place(every, far_up, other, wide.ring(2), core, 0)
        every = place(every, far_down, other, wide.ring(2), core, 1)
    for block, pair, ring in zip(near, (one, one, one, other), (0, 3, 1, 0)):
        every = place(every, halves(block), pair, wide.ring(ring), 1 - wide.at_core)
    every = every.reshape(-1, normed.shape[1])
    every, columns = barrier((every, columns))
    projected = jnp.dot(every, columns, preferred_element_type=jnp.float32).astype(jnp.bfloat16)
    packed = lax.all_to_all(
        projected.reshape(wide_count, rows, -1), "wide", split_axis=0, concat_axis=0, tiled=True
    )
    packed, o_swap, o_up, o_down = barrier((packed, o_swap, o_up, o_down))

    out_rows = w_out.shape[0]
    half_out = out_rows // 2
    o_two_up = wide.up(jnp.concatenate([o_swap, o_up[:half_out]]))
    o_two_down = wide.down(jnp.concatenate([o_swap, o_down[half_out:]]))
    attended = attend(
        packed,
        inverse,
        cosine,
        sine,
        q_gain,
        k_gain,
        stored_keys,
        stored_values,
        span_lengths,
        fill_positions,
    )

    quarter = rows // 4
    attended, w_out, o_up, o_down, o_swap = barrier((attended, w_out, o_up, o_down, o_swap))
    a_up, a_down, a_swap = narrow.up(attended), narrow.down(attended), narrow.swap(attended)
    o_far_up = wide.up(o_two_up[:half_out])
    o_far_down = wide.down(o_two_down[half_out:out_rows])
    (o_near,) = pack(
        (w_out, o_up, o_down, o_swap, o_two_up, o_two_down),
        (
            tuple((i, 0, out_rows) for i in range(4))
            + tuple((i, 0, 3 * half_out) for i in (4, 5)),
        ),
        5,
        6 << 20,
    )
    other_far = jnp.stack([o_far_up, o_far_down])
    a_up, a_down, a_swap, o_far_up, o_far_down, o_near, other_far = barrier(
        (a_up, a_down, a_swap, o_far_up, o_far_down, o_near, other_far)
    )

    low = lax.broadcasted_iota(jnp.int32, (rows, 1), 0) < half_rows
    b_up = narrow.up(jnp.where(low, a_up, a_swap))
    b_down = narrow.down(jnp.where(low, a_swap, a_down))
    b_swap = narrow.swap(jnp.where(low, a_up, a_down))
    o_near = wide.cores(o_near)
    other_far = wide.cores(other_far).reshape(out_rows, -1)
    near_rows = jnp.concatenate([attended, a_swap, a_up, a_down])
    near_rows, o_near, other_far = barrier((near_rows, o_near, other_far))
    chips = tuple(
        (pair * 4 + wide.ring(ring)) * 2
        for ring, pair in (
            (0, wide.at_pair),
            (3, wide.at_pair),
            (1, wide.at_pair),
            (0, 1 - wide.at_pair),
            (3, 1 - wide.at_pair),
            (1, 1 - wide.at_pair),
            (2, wide.at_pair),
            (2, 1 - wide.at_pair),
        )
    )
    every_w_out = put(
        None,
        (w_out, o_up, o_down, o_swap, o_two_up, o_two_down, o_far_up, o_far_down),
        tuple((i, half) for i in range(6) for half in range(2))
        + ((4, 2), (5, 2), (6, 0), (7, 0)),
        jnp.stack([(chip + wide.at_core) * 2 + half for chip in chips for half in range(2)]),
        wide_count * 2,
        half_out,
    )
    every_w_out = put(
        every_w_out,
        (o_near, other_far),
        tuple((0, i) for i in (0, 1, 2, 3, 4, 5, 6, 7, 8, 9, 11, 12, 10, 13)) + ((1, 0), (1, 1)),
        jnp.stack([(chip + 1 - wide.at_core) * 2 + half for chip in chips for half in range(2)]),
        wide_count * 2,
        half_out,
    ).reshape(-1, w_out.shape[1])

    def project_out(part):
        product = jnp.dot(part, every_w_out, preferred_element_type=jnp.float32)
        return product.astype(jnp.bfloat16)

    near_rows = project_out(near_rows)
    b_up, b_down, b_swap, near_rows = barrier((b_up, b_down, b_swap, near_rows))
    c_up = narrow.up(b_up[half_rows : half_rows + quarter])
    c_down = narrow.down(b_swap[half_rows + quarter :])
    c_swap = narrow.swap(b_up[:quarter])
    c_swap_last = narrow.swap(b_up[quarter:half_rows])
    one, other = narrow.at_pair, 1 - narrow.at_pair
    place_of = lambda ring, pair, half: (narrow.ring(ring) * 2 + pair) * 2 + half
    result = order(
        (near_rows, project_out(jnp.concatenate([b_swap, b_up, b_down]))),
        tuple((0, i) for i in range(8)) + tuple((1, i) for i in range(6)),
        jnp.stack(
            [
                place_of(ring, pair, half)
                for ring, pair in ((0, one), (0, other), (3, one), (1, one))
                for half in range(2)
            ]
            + [
                place_of(*place)
                for place in (
                    (3, other, 0),
                    (1, other, 1),
                    (2, one, 0),
                    (3, other, 1),
                    (1, other, 0),
                    (2, one, 1),
                )
            ]
        ),
        16,
        half_rows,
    )
    c_up, c_down, c_swap, c_swap_last, result = barrier(
        (c_up, c_down, c_swap, c_swap_last, result)
    )
    result = put(
        result.reshape(8, rows, -1),
        (project_out(jnp.concatenate([c_swap, c_swap_last, c_up, c_down])),),
        ((0, 0),),
        jnp.stack([narrow.ring(2) * 2 + other]),
        8,
        rows,
    )
    return result.reshape(-1, result.shape[-1])


def solution(mesh):
    placed = (
        P("wide", "narrow"),
        P(),
        P("narrow", "wide"),
        P(),
        P(),
        P(("wide", "narrow"), None, None),
        P(("wide", "narrow"), None, None),
        P(("wide", "narrow")),
        P(("wide", "narrow")),
        P("wide", "narrow"),
    )
    return jax.shard_map(
        shards, mesh=mesh, in_specs=placed, out_specs=P("wide", "narrow"), check_vma=False
    )
```

```python
import functools
import math

import jax
import jax.numpy as jnp
from jax import lax
from jax.experimental import pallas as pl
from jax.experimental.pallas import tpu as pltpu
from jax.sharding import PartitionSpec as P

D = 5120
QUERY_HEADS = 64
KEY_VALUE_HEADS = 8
HEAD_SIZE = 128


EPSILON = 1e-06
ROPE_BASE = 1000000.0


def turn_tables(fill_positions, slots):
    half = HEAD_SIZE // 2
    slot_index = jnp.arange(slots, dtype=jnp.int32)
    position = (fill_positions[:, None] + slot_index[None, :]).reshape(-1).astype(jnp.float32)
    frequency = jnp.exp(
        jnp.arange(half, dtype=jnp.float32) * (-2.0 * math.log(ROPE_BASE) / HEAD_SIZE)
    )
    angles = position[:, None] * frequency[None, :]
    cosine, sine = jnp.cos(angles), jnp.sin(angles)
    return (
        jnp.concatenate([cosine, cosine], axis=1),
        jnp.concatenate([-sine, sine], axis=1),
    )


def attend_kernel(
    fills,
    spans,
    packed,
    inverse,
    cosine,
    sine,
    q_gain,
    k_gain,
    keys,
    values,
    attended,
):
    stream = pl.program_id(0)
    fill, span = fills[stream], spans[stream]
    slots = packed.shape[1]
    frames = keys.shape[1]
    group = QUERY_HEADS // KEY_VALUE_HEADS
    rows = group * slots
    cos_one, sin_one = cosine[...], sine[...]

    def turned(vectors, gains, cos_rows, sin_rows):
        mean_square = jnp.mean(vectors * vectors, axis=-1, keepdims=True)
        normed = vectors * lax.rsqrt(mean_square + EPSILON) * gains
        swapped = pltpu.roll(normed, HEAD_SIZE // 2, 1)
        return (normed * cos_rows + swapped * sin_rows).astype(jnp.bfloat16)

    cos_all = jnp.concatenate([cos_one] * group, axis=0)
    sin_all = jnp.concatenate([sin_one] * group, axis=0)
    low = lax.broadcasted_iota(jnp.int32, (slots, HEAD_SIZE), 1) < HEAD_SIZE // 2
    frame_live = lax.broadcasted_iota(jnp.int32, (rows, frames), 1) < fill
    slot_row = lax.broadcasted_iota(jnp.int32, (group, slots, HEAD_SIZE), 1)
    slot_row = slot_row.reshape(rows, HEAD_SIZE)
    slot_column = lax.broadcasted_iota(jnp.int32, (rows, HEAD_SIZE), 1)
    slot_live = (slot_column <= slot_row) & (slot_column < span)
    row_live = slot_row < span
    empty = jnp.zeros((HEAD_SIZE - slots, HEAD_SIZE), jnp.bfloat16)
    query_columns = group // 2 * HEAD_SIZE
    contract_last = (((1,), (1,)), ((), ()))
    exp_scale = math.log2(math.e) / math.sqrt(HEAD_SIZE)
    def prepare(head):
        queries = jnp.concatenate(
            [
                packed[2 * head + g // 4, :, g % 4 * HEAD_SIZE : (g % 4 + 1) * HEAD_SIZE]
                for g in range(group)
            ],
            axis=0,
        ).astype(jnp.float32)
        queries = turned(queries, q_gain[...], cos_all, sin_all)
        first = packed[2 * head, :, query_columns:].astype(jnp.float32)
        second = packed[2 * head + 1, :, query_columns:].astype(jnp.float32)
        fresh_key = jnp.where(low, first, pltpu.roll(second, HEAD_SIZE // 2, 1))
        fresh_value = jnp.where(low, pltpu.roll(first, HEAD_SIZE // 2, 1), second)
        fresh_key = jnp.concatenate([turned(fresh_key, k_gain[...], cos_one, sin_one), empty])
        fresh_value = jnp.concatenate([(fresh_value * inverse[...]).astype(jnp.bfloat16), empty])
        return queries, fresh_key, fresh_value

    def score(head, queries, fresh_key):
        columns = slice(head * HEAD_SIZE, (head + 1) * HEAD_SIZE)
        old = lax.dot_general(
            queries, keys[0, :, columns], contract_last, preferred_element_type=jnp.float32
        )
        new = lax.dot_general(
            queries, fresh_key, contract_last, preferred_element_type=jnp.float32
        )
        return old, new

    def weigh(old, new):
        old = jnp.where(frame_live, old, -1e30)
        new = jnp.where(slot_live, new, -1e30)
        scores = jnp.concatenate([old, new], axis=1)
        weights = jnp.exp2((scores - jnp.max(scores, axis=-1, keepdims=True)) * exp_scale)
        return weights.astype(jnp.bfloat16), jnp.sum(weights, axis=-1, keepdims=True)

    def mix(head, weights, total, fresh_value):
        columns = slice(head * HEAD_SIZE, (head + 1) * HEAD_SIZE)
        mixed = jnp.dot(
            weights[:, :frames], values[0, :, columns], preferred_element_type=jnp.float32
        ) + jnp.dot(weights[:, frames:], fresh_value, preferred_element_type=jnp.float32)
        mixed = jnp.where(row_live, mixed / total, 0.0).astype(jnp.bfloat16)
        for g in range(group):
            start = (head * group + g) * HEAD_SIZE
            attended[:, start : start + HEAD_SIZE] = mixed[g * slots : (g + 1) * slots]

    for pair in range(0, KEY_VALUE_HEADS, 2):
        heads = (pair, pair + 1)
        prepared = [prepare(head) for head in heads]
        scored = [score(head, p[0], p[1]) for head, p in zip(heads, prepared)]
        weighed = [weigh(*s) for s in scored]
        for head, w, p in zip(heads, weighed, prepared):
            mix(head, *w, p[2])


def attend(packed, inverse, cosine, sine, q_gain, k_gain, keys, values, spans, fills):
    groups, rows, columns = packed.shape
    streams, frames, width = keys.shape
    slots = rows // streams
    heads = QUERY_HEADS * HEAD_SIZE
    tables = pl.BlockSpec((slots, HEAD_SIZE), lambda s, *_: (s, 0))
    gains = pl.BlockSpec((1, HEAD_SIZE), lambda s, *_: (0, 0))
    cache = pl.BlockSpec((1, frames, width), lambda s, *_: (s, 0, 0))
    return pl.pallas_call(
        attend_kernel,
        grid_spec=pltpu.PrefetchScalarGridSpec(
            num_scalar_prefetch=2,
            grid=(streams,),
            in_specs=[
                pl.BlockSpec((groups, slots, columns), lambda s, *_: (0, s, 0)),
                tables,
                tables,
                tables,
                gains,
                gains,
                cache,
                cache,
            ],
            out_specs=pl.BlockSpec((slots, heads), lambda s, *_: (s, 0)),
        ),
        out_shape=jax.ShapeDtypeStruct((rows, heads), jnp.bfloat16),
        compiler_params=pltpu.CompilerParams(vmem_limit_bytes=24 << 20),
        cost_estimate=pl.CostEstimate(
            flops=4 * rows * heads * (frames + slots),
            bytes_accessed=4 * streams * frames * width + 4 * rows * 9216,
            transcendentals=rows * QUERY_HEADS * (frames + slots),
        ),
        name="attend",
    )(
        fills,
        spans,
        packed,
        inverse,
        cosine,
        sine,
        q_gain[None],
        k_gain[None],
        keys,
        values,
    )


class Ring:
    def __init__(self, axis):
        self.axis = axis
        if axis == "narrow":
            self.split = lambda i: (i // 2, i % 2, 0)
        else:
            self.split = lambda i: (i // 2 % 4, i // 8, i % 2)
        self.places = [self.split(i) for i in range(lax.axis_size(axis))]
        index_of = {place: i for i, place in enumerate(self.places)}

        def pairs(steps, flip, core):
            return [
                (i, index_of[((r + steps) % 4, p ^ flip, c ^ core)])
                for i, (r, p, c) in enumerate(self.places)
            ]

        self.pairs = pairs
        self.at_ring, self.at_pair, self.at_core = self.split(lax.axis_index(axis))

    def up(self, block):
        return lax.ppermute(block, self.axis, self.pairs(1, 0, 0))

    def down(self, block):
        return lax.ppermute(block, self.axis, self.pairs(-1, 0, 0))

    def swap(self, block):
        return lax.ppermute(block, self.axis, self.pairs(0, 1, 0))

    def cores(self, block):
        return lax.ppermute(block, self.axis, self.pairs(0, 0, 1))

    def ring(self, steps):
        return (self.at_ring + steps) % 4


def place(buffer, block, *index):
    start = tuple(index) + (0,) * (buffer.ndim - len(index))
    shape = (1,) * (buffer.ndim - block.ndim) + block.shape
    return lax.dynamic_update_slice(buffer, block.reshape(shape), start)


def halves(block):
    return block.reshape((2, -1) + block.shape[1:])


def put_kernel(sources, aliased, places, *refs):
    pieces, result = refs[aliased:-1], refs[-1]
    rows = result.shape[1]
    step = pl.program_id(0)
    for i, (piece, block) in enumerate(sources):

        @pl.when(step == i)
        def _():
            result[0] = pieces[piece][block * rows : (block + 1) * rows]


def put(buffer, pieces, sources, places, blocks, rows, vmem_limit=13 << 20):
    columns = pieces[0].shape[1]
    aliased = 0 if buffer is None else 1
    held = () if buffer is None else (buffer,)
    return pl.pallas_call(
        functools.partial(put_kernel, sources, aliased),
        grid_spec=pltpu.PrefetchScalarGridSpec(
            num_scalar_prefetch=1,
            grid=(len(sources),),
            in_specs=[pl.BlockSpec(memory_space=pl.ANY)] * aliased
            + [pl.BlockSpec(piece.shape, lambda i, *_: (0, 0)) for piece in pieces],
            out_specs=pl.BlockSpec((1, rows, columns), lambda i, places: (places[i], 0, 0)),
        ),
        out_shape=jax.ShapeDtypeStruct((blocks, rows, columns), pieces[0].dtype),
        input_output_aliases={1: 0} if aliased else {},
        compiler_params=pltpu.CompilerParams(vmem_limit_bytes=vmem_limit),
        cost_estimate=pl.CostEstimate(flops=0, bytes_accessed=rows, transcendentals=0),
        name="put",
    )(places, *held, *pieces)


def order_kernel(sources, places, *refs):
    pieces, result = refs[:-1], refs[-1]
    rows = result.shape[1]
    for i, (piece, block) in enumerate(sources):
        result[places[i]] = pieces[piece][block * rows : (block + 1) * rows]


def order(pieces, sources, places, blocks, rows):
    columns = pieces[0].shape[1]
    vmem = pl.BlockSpec(memory_space=pltpu.VMEM)
    return pl.pallas_call(
        functools.partial(order_kernel, sources),
        grid_spec=pltpu.PrefetchScalarGridSpec(
            num_scalar_prefetch=1, in_specs=[vmem] * len(pieces), out_specs=vmem
        ),
        out_shape=jax.ShapeDtypeStruct((blocks, rows, columns), pieces[0].dtype),
        compiler_params=pltpu.CompilerParams(vmem_limit_bytes=8 << 20),
        cost_estimate=pl.CostEstimate(flops=0, bytes_accessed=rows, transcendentals=0),
        name="order",
    )(places, *pieces)


def pack_kernel(payloads, pieces, *refs):
    for payload, out in zip(payloads, refs[pieces:]):
        start = 0
        for piece, source, count in payload:
            out[start : start + count] = refs[piece][source : source + count]
            start += count


def pack(pieces, payloads, steps, vmem_limit=8 << 20):
    columns = pieces[0].shape[1]
    rows = [sum(count for _, _, count in payload) for payload in payloads]
    block = lambda count: pl.BlockSpec((count, columns // steps), lambda i: (0, i))
    return pl.pallas_call(
        functools.partial(pack_kernel, tuple(payloads), len(pieces)),
        grid=(steps,),
        in_specs=[block(piece.shape[0]) for piece in pieces],
        out_specs=[block(count) for count in rows],
        out_shape=[jax.ShapeDtypeStruct((count, columns), pieces[0].dtype) for count in rows],
        compiler_params=pltpu.CompilerParams(vmem_limit_bytes=vmem_limit),
        cost_estimate=pl.CostEstimate(flops=0, bytes_accessed=sum(rows), transcendentals=0),
        name="pack",
    )(*pieces)


def shards(
    tokens,
    ln_gain,
    w_qkv,
    q_gain,
    k_gain,
    stored_keys,
    stored_values,
    span_lengths,
    fill_positions,
    w_out,
):
    barrier = lax.optimization_barrier
    wide, narrow = Ring("wide"), Ring("narrow")
    wide_count = lax.axis_size("wide")
    streams = span_lengths.shape[0]
    rows = tokens.shape[0] // lax.axis_size("narrow")
    slots = rows // streams
    depth = w_qkv.shape[0]
    half_rows, half_depth = rows // 2, depth // 2

    own_rows = lax.all_to_all(tokens, "narrow", split_axis=0, concat_axis=1, tiled=True)
    w_up, w_down, w_swap = narrow.up(w_qkv), narrow.down(w_qkv), narrow.swap(w_qkv)
    o_up, o_down = wide.up(w_out), wide.down(w_out)
    token_values = own_rows.astype(jnp.float32)
    own_squares = jnp.sum(token_values * token_values, axis=1)
    normed = (token_values * ln_gain[None, :]).astype(jnp.bfloat16)
    o_up, o_down, w_swap, w_up, w_down, normed = barrier(
        (o_up, o_down, w_swap, w_up, w_down, normed)
    )

    w_swap_up, w_swap_down = narrow.up(w_swap), narrow.down(w_swap)
    t_up, t_down, t_swap = wide.up(normed), wide.down(normed), wide.swap(normed)
    inverse = jnp.broadcast_to(lax.rsqrt(own_squares / D + EPSILON)[:, None], (rows, HEAD_SIZE))
    cosine, sine = turn_tables(fill_positions, slots)
    one, other = wide.at_pair, 1 - wide.at_pair
    every = jnp.zeros((2, 4, 2, 2, half_rows) + normed.shape[1:], normed.dtype)
    every = place(every, halves(normed), one, wide.ring(0), wide.at_core)
    w_swap_up, w_swap_down, t_up, t_down, t_swap, inverse, cosine, sine, every = barrier(
        (w_swap_up, w_swap_down, t_up, t_down, t_swap, inverse, cosine, sine, every)
    )

    w_far_up = narrow.up(jnp.concatenate([w_up[:half_depth], w_swap_up[:half_depth]]))
    w_far_down = narrow.down(jnp.concatenate([w_down[half_depth:], w_swap_down[half_depth:]]))
    t_two_up = wide.up(jnp.concatenate([t_swap, t_up[:half_rows]]))
    t_two_down = wide.down(jnp.concatenate([t_swap, t_down[half_rows:]]))
    o_swap = wide.swap(w_out)
    near = jnp.stack([normed, t_up, t_down, t_swap])
    at_narrow = tuple(
        narrow.ring(ring) * 2 + pair
        for pair in (narrow.at_pair, 1 - narrow.at_pair)
        for ring in (0, 3, 1, 2)
    )
    columns = put(
        None,
        (w_qkv, w_up, w_down, w_swap, w_swap_up, w_swap_down),
        tuple((i, half) for i in range(6) for half in range(2)),
        jnp.stack([at_narrow[i] * 2 + half for i in (0, 1, 2, 4, 5, 6) for half in range(2)]),
        16,
        half_depth,
    )
    every = place(every, halves(t_up), one, wide.ring(3), wide.at_core)
    every = place(every, halves(t_down), one, wide.ring(1), wide.at_core)
    every = place(every, halves(t_swap), other, wide.ring(0), wide.at_core)
    w_far_up, w_far_down, t_two_up, t_two_down, o_swap, near, columns, every = barrier(
        (w_far_up, w_far_down, t_two_up, t_two_down, o_swap, near, columns, every)
    )

    t_far_up = wide.up(t_two_up[:half_rows])
    t_far_down = wide.down(t_two_down[half_rows:rows])
    near = wide.cores(near)
    two = wide.cores(jnp.stack([t_two_up, t_two_down]))
    far = wide.cores(jnp.stack([t_far_up, t_far_down]))
    columns = put(
        columns,
        (w_far_up, w_far_down),
        ((0, 0), (1, 0), (0, 1), (1, 1)),
        jnp.stack([at_narrow[i] * 2 + half for i in (3, 7) for half in range(2)]),
        16,
        half_depth,
    ).reshape(-1, w_qkv.shape[1])
    for core, (two_up, two_down), (far_up, far_down) in (
        (wide.at_core, (t_two_up, t_two_down), (t_far_up, t_far_down)),
        (1 - wide.at_core, two, far),
    ):
        every = place(every, halves(two_up[:rows]), other, wide.ring(3), core)
        every = place(every, halves(two_down[:rows]), other, wide.ring(1), core)
        every = place(every, two_up[rows:], one, wide.ring(2), core, 0)
        every = place(every, two_down[rows:], one, wide.ring(2), core, 1)
        every = place(every, far_up, other, wide.ring(2), core, 0)
        every = place(every, far_down, other, wide.ring(2), core, 1)
    for block, pair, ring in zip(near, (one, one, one, other), (0, 3, 1, 0)):
        every = place(every, halves(block), pair, wide.ring(ring), 1 - wide.at_core)
    every = every.reshape(-1, normed.shape[1])
    every, columns = barrier((every, columns))
    projected = jnp.dot(every, columns, preferred_element_type=jnp.float32).astype(jnp.bfloat16)
    packed = lax.all_to_all(
        projected.reshape(wide_count, rows, -1), "wide", split_axis=0, concat_axis=0, tiled=True
    )
    packed, o_swap, o_up, o_down = barrier((packed, o_swap, o_up, o_down))

    out_rows = w_out.shape[0]
    half_out = out_rows // 2
    o_two_up = wide.up(jnp.concatenate([o_swap, o_up[:half_out]]))
    o_two_down = wide.down(jnp.concatenate([o_swap, o_down[half_out:]]))
    attended = attend(
        packed,
        inverse,
        cosine,
        sine,
        q_gain,
        k_gain,
        stored_keys,
        stored_values,
        span_lengths,
        fill_positions,
    )

    quarter = rows // 4
    attended, w_out, o_up, o_down, o_swap = barrier((attended, w_out, o_up, o_down, o_swap))
    a_up, a_down, a_swap = narrow.up(attended), narrow.down(attended), narrow.swap(attended)
    o_far_up = wide.up(o_two_up[:half_out])
    o_far_down = wide.down(o_two_down[half_out:out_rows])
    (o_near,) = pack(
        (w_out, o_up, o_down, o_swap, o_two_up, o_two_down),
        (
            tuple((i, 0, out_rows) for i in range(4))
            + tuple((i, 0, 3 * half_out) for i in (4, 5)),
        ),
        5,
        6 << 20,
    )
    other_far = jnp.stack([o_far_up, o_far_down])
    a_up, a_down, a_swap, o_far_up, o_far_down, o_near, other_far = barrier(
        (a_up, a_down, a_swap, o_far_up, o_far_down, o_near, other_far)
    )

    b_up = narrow.up(jnp.concatenate([a_swap[half_rows:], a_up[:half_rows]]))
    b_down = narrow.down(jnp.concatenate([a_swap[half_rows:], a_down[half_rows:]]))
    b_swap = narrow.swap(jnp.concatenate([a_up[:half_rows], a_down[:half_rows]]))
    o_near = wide.cores(o_near)
    other_far = wide.cores(other_far).reshape(out_rows, -1)
    near_rows = jnp.concatenate([attended, a_swap, a_up, a_down])
    near_rows, o_near, other_far = barrier((near_rows, o_near, other_far))
    chips = tuple(
        (pair * 4 + wide.ring(ring)) * 2
        for ring, pair in (
            (0, wide.at_pair),
            (3, wide.at_pair),
            (1, wide.at_pair),
            (0, 1 - wide.at_pair),
            (3, 1 - wide.at_pair),
            (1, 1 - wide.at_pair),
            (2, wide.at_pair),
            (2, 1 - wide.at_pair),
        )
    )
    every_w_out = put(
        None,
        (w_out, o_up, o_down, o_swap, o_two_up, o_two_down, o_far_up, o_far_down),
        tuple((i, half) for i in range(6) for half in range(2))
        + ((4, 2), (5, 2), (6, 0), (7, 0)),
        jnp.stack([(chip + wide.at_core) * 2 + half for chip in chips for half in range(2)]),
        wide_count * 2,
        half_out,
    )
    every_w_out = put(
        every_w_out,
        (o_near, other_far),
        tuple((0, i) for i in (0, 1, 2, 3, 4, 5, 6, 7, 8, 9, 11, 12, 10, 13)) + ((1, 0), (1, 1)),
        jnp.stack([(chip + 1 - wide.at_core) * 2 + half for chip in chips for half in range(2)]),
        wide_count * 2,
        half_out,
    ).reshape(-1, w_out.shape[1])

    def project_out(part):
        product = jnp.dot(part, every_w_out, preferred_element_type=jnp.float32)
        return product.astype(jnp.bfloat16)

    near_rows = project_out(near_rows)
    b_up, b_down, b_swap, near_rows = barrier((b_up, b_down, b_swap, near_rows))
    c_up = narrow.up(b_up[:quarter])
    c_down = narrow.down(b_down[quarter:half_rows])
    c_swap = narrow.swap(b_up[half_rows : half_rows + quarter])
    c_swap_last = narrow.swap(b_up[half_rows + quarter :])
    one, other = narrow.at_pair, 1 - narrow.at_pair
    place_of = lambda ring, pair, half: (narrow.ring(ring) * 2 + pair) * 2 + half
    result = order(
        (near_rows, project_out(jnp.concatenate([b_swap, b_up, b_down]))),
        tuple((0, i) for i in range(8)) + tuple((1, i) for i in range(6)),
        jnp.stack(
            [
                place_of(ring, pair, half)
                for ring, pair in ((0, one), (0, other), (3, one), (1, one))
                for half in range(2)
            ]
            + [
                place_of(*place)
                for place in (
                    (3, other, 0),
                    (1, other, 0),
                    (3, other, 1),
                    (2, one, 0),
                    (1, other, 1),
                    (2, one, 1),
                )
            ]
        ),
        16,
        half_rows,
    )
    c_up, c_down, c_swap, c_swap_last, result = barrier(
        (c_up, c_down, c_swap, c_swap_last, result)
    )
    result = put(
        result.reshape(8, rows, -1),
        (project_out(jnp.concatenate([c_swap, c_swap_last, c_up, c_down])),),
        ((0, 0),),
        jnp.stack([narrow.ring(2) * 2 + other]),
        8,
        rows,
    )
    return result.reshape(-1, result.shape[-1])


def solution(mesh):
    placed = (
        P("wide", "narrow"),
        P(),
        P("narrow", "wide"),
        P(),
        P(),
        P(("wide", "narrow"), None, None),
        P(("wide", "narrow"), None, None),
        P(("wide", "narrow")),
        P(("wide", "narrow")),
        P("wide", "narrow"),
    )
    return jax.shard_map(
        shards, mesh=mesh, in_specs=placed, out_specs=P("wide", "narrow"), check_vma=False
    )
```
